512 devices in a mesh: seq: 16 (over z), tensor: 4 (over y), dp: 8 (over x, core).
Axes of the slice: x: 4, y: 4, z: 16, core: 2. Of those that a mesh axis runs over, the one named last changes fastest.
Arguments:
- seq_values: bfloat16 [8, 2048, 8192], P('dp', 'seq', 'tensor'), may hold values from -6 to 6
- proj_b: bfloat16 [8, 2048, 512], P('dp', 'seq', 'tensor'), may hold values from -0.75 to 0.75
- proj_c: bfloat16 [8, 2048, 512], P('dp', 'seq', 'tensor'), may hold values from -0.75 to 0.75
- time_step: float32 [8, 2048, 128], P('dp', 'seq', 'tensor'), may hold values from 0.5 to 6144, as said below
- decay_level: int32 [8, 16, 128], P('dp', 'seq', 'tensor'), may hold values from 0 to 7
- decay_rate: float32 [128, 8], P('tensor'), may hold values from 4.8828125e-05 to 0.06666667, as said below
- skip_gain: float32 [128], P('tensor'), may hold values from 0.5 to 2
- grad_out: bfloat16 [8, 2048, 8192], P('dp', 'seq', 'tensor'), may hold values from -12 to 12
- layer_input: bfloat16 [8, 2048, 8192], P('dp', 'seq', 'tensor'), may hold values from -64 to 64
- weight_c: float32 [8192, 512], P(('seq', 'dp'), 'tensor'), may hold values from -0.75 to 0.75
- moment_one: float32 [8192, 512], P(('seq', 'dp'), 'tensor'), may hold values from -4 to 4
- moment_two: float32 [8192, 512], P(('seq', 'dp'), 'tensor'), may hold values from 0.01 to 0.1
Outputs:
- grad_values: bfloat16 [8, 2048, 8192], P('dp', 'seq', 'tensor')
- grad_b: bfloat16 [8, 2048, 512], P('dp', 'seq', 'tensor')
- grad_c: bfloat16 [8, 2048, 512], P('dp', 'seq', 'tensor')
- grad_lograte: float32 [128, 8], P('tensor')
- grad_skip: float32 [128], P('tensor')
- new_weight: float32 [8192, 512], P(('seq', 'dp'), 'tensor')
- new_moment: float32 [8192, 512], P(('seq', 'dp'), 'tensor')
- new_second: float32 [8192, 512], P(('seq', 'dp'), 'tensor')
The draws below stay inside these ranges and needn't reach their ends.
Inputs may be any that keep to these rules, and one draw needn't show every extreme that they name: `decay_rate`: positive decay rates. `time_step`: positive step sizes.
All inputs are finite; a program needn't handle non-finite values.
Results may differ from the reference program's by a relative error of at most 0.015.
Values may be sent and summed in bfloat16 or wider, within the bound.
No kernel may reach another device: no remote copies, remote signals or barrier semaphores. Data moves between devices by JAX's collectives and lax.ppermute only.
A program may use at most 128 MiB of HBM per device.

```python
import math
from functools import partial
import jax
import jax.numpy as jnp
from jax import lax

D = 8192
MIXER_CHANNELS = 128
P_SIZE = 64
N = 128
G = 4
LEVELS = 8
LEVEL_SPAN = 128
LEN = 2048
STREAM_COUNT = 8


def channel_decays(key):
    key_fast, key_slow, key_quick = jax.random.split(jax.random.fold_in(key, 11), 3)
    share = 0.5
    fast = jax.random.uniform(key_fast, (MIXER_CHANNELS,)) < share
    slow_rate = jax.random.uniform(key_slow, (MIXER_CHANNELS,), minval=0.1, maxval=0.4) / LEN
    quick_rate = jnp.exp(jax.random.uniform(key_quick, (MIXER_CHANNELS,), minval=math.log(0.0025), maxval=math.log(1.0 / 30.0)))
    return jnp.where(fast, quick_rate, slow_rate)


def draw_decay_rate(key, part):
    factor = jnp.exp(jax.random.uniform(jax.random.fold_in(key, 12), (MIXER_CHANNELS, LEVELS), minval=0.0, maxval=math.log(2.0)))
    return (channel_decays(key)[:, None] * factor).astype(jnp.float32)


def draw_time_step(key, part):
    base_key, place_key, length_seed = jax.random.split(jax.random.fold_in(key, 13), 3)
    lower = 0.5
    upper = 1.5
    starting_shift = jax.random.uniform(base_key, (STREAM_COUNT, LEN, MIXER_CHANNELS), minval=lower, maxval=upper)
    places = jax.random.randint(place_key, (STREAM_COUNT, 2, MIXER_CHANNELS), 0, LEN)
    positions = jnp.arange(LEN, dtype=jnp.int32)[None, :, None]
    masked_items = (positions == places[:, 0:1, :]) | (positions == places[:, 1:2, :])
    spike_multiplier = jax.random.uniform(length_seed, (STREAM_COUNT, 1, MIXER_CHANNELS), minval=0.15, maxval=0.3) / channel_decays(key)[None, None, :]
    return jnp.where(masked_items, spike_multiplier, starting_shift).astype(jnp.float32)


def draw_grad_out(key, part):
    noise_key = jax.random.fold_in(jax.random.fold_in(key, 14), 0)
    ramp = jnp.exp(math.log(3.0) * jnp.arange(LEN, dtype=jnp.float32) / (LEN - 1))[None, :, None]
    noise = jnp.clip(jax.random.normal(noise_key, (STREAM_COUNT, LEN, MIXER_CHANNELS * P_SIZE)), -4.0, 4.0)
    row_scale = jnp.ones((STREAM_COUNT, LEN, 1), jnp.float32)
    return (0.1 * ramp * row_scale * noise).astype(jnp.bfloat16)


def draw_layer_input(key, part):
    noise_key = jax.random.fold_in(jax.random.fold_in(key, 15), 0)
    level_key = jax.random.fold_in(jax.random.fold_in(key, 15), 2)
    ramp = jnp.exp(math.log(3.0) * jnp.arange(D, dtype=jnp.float32) / (D - 1))
    block_ids = jnp.arange(D, dtype=jnp.int32) * 32 // D
    block_levels = jnp.exp(jax.random.uniform(level_key, (32,), minval=-1.0, maxval=1.0))
    feature_scale = (ramp * block_levels[block_ids])[None, None, :]
    noise = jnp.clip(jax.random.normal(noise_key, (STREAM_COUNT, LEN, D)), -4.0, 4.0)
    row_scale = jnp.ones((STREAM_COUNT, LEN, 1), jnp.float32)
    return (feature_scale * row_scale * noise).astype(jnp.bfloat16)


def set_ends(values, key, least, high):
    longest = values.shape.index(max(values.shape))
    spots = []
    for shift in (0, 1):
        where = [jax.random.randint(jax.random.fold_in(key, axis), (), 0, length) for axis, length in enumerate(values.shape)]
        where[longest] = (where[longest] + shift) % values.shape[longest]
        spots.append(tuple(where))
    return values.at[spots[0]].set(least).at[spots[1]].set(high)


def shard_levels(stream_key, dims, cuts, smallest, largest):
    def one(position, parts):
        heights = jax.random.uniform(jax.random.fold_in(jax.random.fold_in(stream_key, 6), position), (parts,), jnp.float32, smallest / len(cuts), largest / len(cuts))
        return jnp.repeat(jnp.exp(heights), dims[position] // parts).reshape((-1,) + (1,) * (len(dims) - position - 1))

    gain = one(*cuts[0])
    for cut in cuts[1:]:
        gain = gain * one(*cut)
    return gain


def normal_values(rng, dims, deviation, reach, shards=(), kind=jnp.bfloat16):
    values = jax.random.normal(rng, dims, jnp.float32) * deviation
    if len(shards) > 0:
        values = shard_levels(rng, dims, shards, -0.22, 0.18) * values
    return jnp.clip(values, min=-reach, max=reach).astype(kind)


def setup_inputs(seed: int = 0) -> dict:
    key_list = jax.random.split(jax.random.key(seed), 13)
    return {
        "seq_values": normal_values(key_list[0], (STREAM_COUNT, LEN, MIXER_CHANNELS * P_SIZE), 1.0, 6.0, ((0, 8), (1, 16), (2, 4))),
        "proj_b": normal_values(key_list[1], (STREAM_COUNT, LEN, G * N), 0.05, 0.75, ((0, 8), (1, 16), (2, 4))),
        "proj_c": normal_values(key_list[2], (STREAM_COUNT, LEN, G * N), 0.05, 0.75, ((0, 8), (1, 16), (2, 4))),
        "time_step": draw_time_step(jax.random.fold_in(key_list[12], 71), 0),
        "decay_level": set_ends(jax.random.randint(key_list[4], (STREAM_COUNT, LEN // LEVEL_SPAN, MIXER_CHANNELS), 0, LEVELS), jax.random.fold_in(key_list[4], 1), 0, LEVELS - 1).astype(jnp.int32),
        "decay_rate": draw_decay_rate(jax.random.fold_in(key_list[12], 71), 0),
        "skip_gain": jnp.clip(0.5 + 1.5 * jax.random.uniform(key_list[6], (MIXER_CHANNELS,), jnp.float32) ** shard_levels(key_list[6], (MIXER_CHANNELS,), ((0, 4),), -0.2, 0.2), 0.5, 2.0),
        "grad_out": draw_grad_out(jax.random.fold_in(key_list[12], 71), 0),
        "layer_input": draw_layer_input(jax.random.fold_in(key_list[12], 71), 0),
        "weight_c": normal_values(key_list[9], (D, G * N), 0.05, 0.75, ((0, 128), (1, 4)), jnp.float32),
        "moment_one": normal_values(key_list[10], (D, G * N), 0.25, 4.0, ((0, 128), (1, 4)), jnp.float32),
        "moment_two": jnp.clip(jnp.exp(math.log(0.1) - 2.3025851 * jax.random.uniform(key_list[11], (D, G * N), jnp.float32) ** shard_levels(key_list[11], (D, G * N), ((0, 128), (1, 4)), -0.2, 0.2)), 0.01, 0.1),
    }


beta_one = 0.9
beta_two = 0.95
adam_eps = 1e-08
learn_rate = 0.02
decay_weight = 0.1
step_count = 10

def block_forward(skip_gain, state, pieces):
    values, b_rows, c_rows, log_decay = pieces
    block_len = values.shape[0]
    per_group = values.shape[1] // b_rows.shape[1]
    cumulative = jnp.cumsum(log_decay, axis=0)
    b_heads = jnp.repeat(b_rows, per_group, axis=1)
    c_heads = jnp.repeat(c_rows, per_group, axis=1)
    gram = jnp.repeat(jnp.einsum('tgn,sgn->gts', c_rows, b_rows), per_group, axis=0)
    row_ids = lax.broadcasted_iota(jnp.int32, (1, block_len, block_len), 1)
    col_ids = lax.broadcasted_iota(jnp.int32, (1, block_len, block_len), 2)
    diff = cumulative.T[:, :, None] - cumulative.T[:, None, :]
    weights = jnp.where(row_ids >= col_ids, jnp.exp(jnp.minimum(diff, 0.0)), 0.0) * gram
    output = jnp.einsum('hts,shp->thp', weights, values)
    carried = jnp.exp(cumulative)[:, :, None] * jnp.einsum('thn,hnp->thp', c_heads, state)
    output = output + carried + skip_gain[None, :, None] * values
    last_cum = cumulative[-1]
    tail = jnp.exp(last_cum[None, :] - cumulative)
    new_state = jnp.exp(last_cum)[:, None, None] * state + jnp.einsum('thn,th,thp->hnp', b_heads, tail, values)
    return (new_state, output)

def row_forward(values, b_rows, c_rows, log_decay, skip_gain):
    block_count = values.shape[0] // LEVEL_SPAN

    def to_blocks(array):
        return array.reshape((block_count, LEVEL_SPAN) + array.shape[1:])
    zero_state = jnp.zeros((values.shape[1], N, P_SIZE), values.dtype)
    _, outputs = lax.scan(partial(block_forward, skip_gain), zero_state, (to_blocks(values), to_blocks(b_rows), to_blocks(c_rows), to_blocks(log_decay)))
    return outputs.reshape(values.shape)

def reference(seq_values, proj_b, proj_c, time_step, decay_level, decay_rate, skip_gain, grad_out, layer_input, weight_c, moment_one, moment_two):
    tok_level = jnp.repeat(decay_level, LEVEL_SPAN, axis=1)
    level_ids = jnp.arange(LEVELS, dtype=jnp.int32)
    onehot = (tok_level[..., None] == level_ids).astype(jnp.float32)
    tok_rate = lax.optimization_barrier(jnp.sum(onehot * decay_rate[None, None], axis=3))
    log_decay = -tok_rate * time_step

    def row_grads(packed):
        row_values, row_b, row_c, row_decay, row_grad = packed
        _, pullback = jax.vjp(row_forward, row_values.astype(jnp.float32).reshape(LEN, MIXER_CHANNELS, P_SIZE), row_b.astype(jnp.float32).reshape(LEN, G, N), row_c.astype(jnp.float32).reshape(LEN, G, N), row_decay, skip_gain)
        return pullback(row_grad.astype(jnp.float32).reshape(LEN, MIXER_CHANNELS, P_SIZE))
    d_values, d_b, d_c, d_decay, d_skip = lax.map(row_grads, (seq_values, proj_b, proj_c, log_decay, grad_out))
    grad_values = d_values.reshape(STREAM_COUNT, LEN, MIXER_CHANNELS * P_SIZE).astype(jnp.bfloat16)
    grad_b = d_b.reshape(STREAM_COUNT, LEN, G * N).astype(jnp.bfloat16)
    grad_c = d_c.reshape(STREAM_COUNT, LEN, G * N).astype(jnp.bfloat16)
    grad_lograte = lax.optimization_barrier(jnp.sum(onehot * (d_decay * log_decay)[..., None], axis=(0, 1)))
    grad_skip = lax.optimization_barrier(jnp.sum(d_skip, axis=0))
    weight_grad = lax.dot_general(layer_input.reshape(STREAM_COUNT * LEN, D), grad_c.reshape(STREAM_COUNT * LEN, G * N), (((0,), (0,)), ((), ())), preferred_element_type=jnp.float32)
    limit = 0.25 * math.sqrt(D * G * N)
    norm_value = jnp.sqrt(jnp.sum(weight_grad * weight_grad))
    clipped = weight_grad * (limit / jnp.maximum(norm_value, limit))
    new_moment = beta_one * moment_one + (1.0 - beta_one) * clipped
    new_second = beta_two * moment_two + (1.0 - beta_two) * clipped * clipped
    direction = new_moment / (1.0 - beta_one ** step_count) / (jnp.sqrt(new_second / (1.0 - beta_two ** step_count)) + adam_eps)
    new_weight = weight_c - learn_rate * (direction + decay_weight * weight_c)
    return (grad_values, grad_b, grad_c, grad_lograte, grad_skip, new_weight, new_moment, new_second)
```

```python
import math

import jax
import jax.numpy as jnp
from jax import lax
from jax.experimental import pallas as pl
from jax.experimental.pallas import tpu as pltpu
from jax.sharding import PartitionSpec as P

P_SIZE = 64
N = 128
SPAN = 128
PAIR = 2 * P_SIZE
LOG_ROWS = 16

beta_one = 0.9
beta_two = 0.95
adam_eps = 1e-08
learn_rate = 0.02
decay_weight = 0.1
step_count = 10

f32 = jnp.float32
bf16 = jnp.bfloat16
HIGHEST = lax.Precision.HIGHEST


def iota(shape, dim):
    return lax.broadcasted_iota(jnp.int32, shape, dim)


def dot(a, b):
    return jnp.dot(a, b, preferred_element_type=f32)


def dot_nt(a, b):
    return lax.dot_general(a, b, (((1,), (1,)), ((), ())), preferred_element_type=f32)


def first_head():
    return iota((SPAN, PAIR), 1) < P_SIZE


def spread(cols, j, first):
    return jnp.where(
        first[: cols.shape[0]], cols[:, 2 * j : 2 * j + 1], cols[:, 2 * j + 1 : 2 * j + 2]
    )


def states_kernel(dt, lev, rate_t, x, dy, b, c, st, xt, dye, loga, cum, onehot):
    heads = dt.shape[1]
    levels = rate_t.shape[0]
    hit = iota((levels, heads), 0) == lev[...]
    rate = jnp.sum(jnp.where(hit, rate_t[...], 0.0), axis=0, keepdims=True)
    onehot[...] = jnp.zeros_like(onehot)
    onehot[:, :heads] = jnp.where(hit, 1.0, 0.0)
    loga[...] = jnp.zeros_like(loga)
    loga[:, :heads] = -rate * dt[...]
    lower = (iota((SPAN, SPAN), 0) >= iota((SPAN, SPAN), 1)).astype(f32)
    total = jnp.dot(lower, loga[...], precision=HIGHEST, preferred_element_type=f32)
    cum[...] = total
    last = total[SPAN - 1 :, :]
    tail = jnp.exp(last - total)
    grow = jnp.exp(total)
    b_t = b[...].astype(f32).T.astype(bf16)
    c_t = c[...].astype(f32).T.astype(bf16)
    first = first_head()
    row = iota((LOG_ROWS, PAIR), 0)
    heads_piece = PAIR // P_SIZE * (heads // 2) // st.shape[0]
    for j in range(heads // 2):
        piece, at = 2 * j // heads_piece, (2 * j % heads_piece) // 2 * PAIR
        lanes = slice(j * PAIR, (j + 1) * PAIR)
        spot = slice(at, at + PAIR)
        xs = (x[:, lanes].astype(f32) * spread(tail, j, first)).astype(bf16)
        ds = (dy[:, lanes].astype(f32) * spread(grow, j, first)).astype(bf16)
        xt[:, lanes] = xs
        dye[:, lanes] = ds
        st[piece, :N, spot] = dot(b_t, xs).astype(bf16)
        st[piece, N : 2 * N, spot] = dot(c_t, ds).astype(bf16)
        whole = spread(last, j, first)
        high = whole.astype(bf16).astype(f32)
        middle = (whole - high).astype(bf16).astype(f32)
        low = whole - high - middle
        st[piece, 2 * N :, spot] = jnp.where(
            row == 0, high, jnp.where(row == 1, middle, jnp.where(row == 2, low, 0.0))
        ).astype(bf16)


def scan_kernel(got, starts, ends):
    count = got.shape[0]
    decay = []
    for k in range(count):
        logs = got[k, 2 * N :, :].astype(f32)
        decay.append(jnp.exp(logs[0:1] + logs[1:2] + logs[2:3]))
    state = jnp.zeros((N, got.shape[2]), f32)
    for k in range(count):
        starts[k] = state.astype(bf16)
        state = decay[k] * state + got[k, :N, :].astype(f32)
    state = jnp.zeros((N, got.shape[2]), f32)
    for k in reversed(range(count)):
        ends[k] = state.astype(bf16)
        state = decay[k] * state + got[k, N : 2 * N, :].astype(f32)


def intra_kernel(cum, x, dy, b, c, skip, dxp, dc, db, dcum, rows):
    heads = skip.shape[1]
    total = cum[...]
    total_t = total.T
    keep = iota((SPAN, SPAN), 1) >= iota((SPAN, SPAN), 0)
    lane = iota((SPAN, SPAN), 1)
    first = first_head()
    gain = skip[...]
    mask_a = jnp.where(first, 1.0, 0.0).astype(bf16)
    mask_b = jnp.where(first, 0.0, 1.0).astype(bf16)
    gram_t = dot_nt(b[...], c[...])
    dgram_t = jnp.zeros((SPAN, SPAN), f32)
    columns = jnp.zeros((SPAN, SPAN), f32)
    rows[...] = jnp.zeros_like(rows)
    for j in range(heads // 2):
        lanes = slice(j * PAIR, (j + 1) * PAIR)
        x_pair, dy_pair = x[:, lanes], dy[:, lanes]
        x_two = jnp.concatenate([x_pair * mask_a, x_pair * mask_b], axis=0)
        dy_two = jnp.concatenate([dy_pair * mask_a, dy_pair * mask_b], axis=0)
        dm_two = dot_nt(x_two, dy_pair)
        mixes = []
        for k in range(2):
            h = 2 * j + k
            dm = dm_two[k * SPAN : (k + 1) * SPAN]
            diff = total_t[h : h + 1, :] - total[:, h : h + 1]
            w = jnp.exp(jnp.where(keep, jnp.minimum(diff, 0.0), -1e30))
            wd = w * dm
            dgram_t = dgram_t + wd
            q = wd * gram_t
            columns = jnp.where(lane == h, jnp.sum(q, axis=1, keepdims=True), columns)
            rows[h : h + 1, :] = jnp.sum(q, axis=0, keepdims=True)
            mixes.append((w * gram_t).astype(bf16))
        dx = dot(jnp.concatenate(mixes, axis=1), dy_two)
        dxp[:, lanes] = dx + spread(gain, j, first) * dy_pair.astype(f32)
    dcum[...] = rows[...].T - columns
    high = dgram_t.astype(bf16)
    dc[...] = dot(high.astype(f32).T.astype(bf16), b[...])
    db[...] = dot(high, c[...])


def grad_c_kernel(dc, dye, starts, grad_c, copies):
    total = dc[...]
    pieces, width = starts.shape[0], starts.shape[2]
    for j in range(pieces):
        total = total + dot_nt(dye[:, j * width : (j + 1) * width], starts[j])
    out = total.astype(bf16)
    grad_c[...] = out
    for k in range(copies.shape[0]):
        copies[k] = out


def halves(a):
    high = a.astype(bf16)
    return high, (a - high.astype(f32)).astype(bf16)


def rest_kernel(
    starts, ends, x, dy, xt, dye, cum, loga, onehot, b, c, dxp, db, dcum, grad_x, grad_b, small
):
    heads = x.shape[1] // P_SIZE
    pairs_piece = starts.shape[2] // PAIR
    total = cum[...]
    last = total[SPAN - 1 :, :]
    tail = jnp.exp(last - total)
    end = jnp.exp(last)
    first = first_head()
    row = iota((SPAN, PAIR), 0)
    lane_head = iota((PAIR, 128), 0) // P_SIZE
    column = iota((PAIR, 128), 1)
    b_total = db[...]
    d_total = dcum[...]
    skips = jnp.zeros((8, 128), f32)
    for j in range(heads // 2):
        piece, at = j // pairs_piece, j % pairs_piece * PAIR
        lanes = slice(j * PAIR, (j + 1) * PAIR)
        start, stop = starts[piece, :, at : at + PAIR], ends[piece, :, at : at + PAIR]
        xs = xt[:, lanes]
        carried = dye[:, lanes].astype(f32) * dot(c[...], start)
        back = dot(b[...], stop)
        left = xs.astype(f32) * back
        grad_x[:, lanes] = (dxp[:, lanes] + spread(tail, j, first) * back).astype(bf16)
        b_total = b_total + dot_nt(xs, stop)
        at_end = jnp.sum(left, axis=0, keepdims=True) + spread(end, j, first) * jnp.sum(
            start.astype(f32) * stop.astype(f32), axis=0, keepdims=True
        )
        moved = carried - left + jnp.where(row == SPAN - 1, at_end, 0.0)
        skip = jnp.sum(x[:, lanes].astype(f32) * dy[:, lanes].astype(f32), axis=0, keepdims=True)
        skip = jnp.broadcast_to(skip, (8, PAIR))
        to_head = jnp.where(column == 2 * j + lane_head, 1.0, 0.0).astype(bf16)
        to_skip = jnp.where(column == heads + 2 * j + lane_head, 1.0, 0.0).astype(bf16)
        high, low = halves(moved)
        d_total = d_total + dot(high, to_head) + dot(low, to_head)
        high, low = halves(skip)
        skips = skips + dot(high, to_skip) + dot(low, to_skip)
    grad_b[...] = b_total.astype(bf16)
    upper = (iota((SPAN, SPAN), 1) >= iota((SPAN, SPAN), 0)).astype(f32)
    dlog = jnp.dot(upper, d_total, precision=HIGHEST, preferred_element_type=f32)
    rates = jnp.sum(dlog * loga[...], axis=0, keepdims=True)
    small[...] = onehot[...] * rates + jnp.where(iota((8, 128), 0) == 0, skips, 0.0)


def shard_kernel(parts, small, shard, copies):
    total = jnp.sum(parts[...].astype(f32), axis=0)
    shard[...] = total
    square = jnp.sum(total * total)
    here = (iota((8, 128), 0) == 0) & (iota((8, 128), 1) == 127)
    out = small[...] + jnp.where(here, square, 0.0)
    for k in range(copies.shape[0]):
        copies[k] = out


def call(kernel, out_shapes, *args, scratch=(), flops=0):
    size = sum(math.prod(a.shape) * a.dtype.itemsize for a in (*args, *out_shapes))
    return pl.pallas_call(
        kernel,
        out_shape=tuple(out_shapes),
        scratch_shapes=list(scratch),
        compiler_params=pltpu.CompilerParams(vmem_limit_bytes=48 * 1024 * 1024),
        cost_estimate=pl.CostEstimate(flops=flops, bytes_accessed=size, transcendentals=0),
    )(*args)


def shaped(shape, dtype):
    return jax.ShapeDtypeStruct(shape, dtype)


def swap(a, axis):
    return lax.all_to_all(a, axis, 0, 0, tiled=True)


def local(
    seq_values,
    proj_b,
    proj_c,
    time_step,
    decay_level,
    decay_rate,
    skip_gain,
    grad_out,
    layer_input,
    weight_c,
    moment_one,
    moment_two,
):
    seqs, streams, tensors = (lax.axis_size(a) for a in ("seq", "dp", "tensor"))
    x, dy, b, c = seq_values[0], grad_out[0], proj_b[0], proj_c[0]
    heads = skip_gain.shape[0]
    width = heads * P_SIZE
    piece = width // seqs
    tile = shaped((SPAN, 128), f32)
    wide = shaped((SPAN, width), bf16)
    st, xt, dye, loga, cum, onehot = call(
        states_kernel,
        [shaped((seqs, 2 * N + LOG_ROWS, piece), bf16), wide, wide, tile, tile, shaped((8, 128), f32)],
        time_step[0],
        decay_level[0],
        decay_rate.T,
        x,
        dy,
        b,
        c,
        flops=4 * SPAN * N * width,
    )
    got = swap(st, "seq")

    rows = weight_c.shape[0]
    per_tensor = layer_input.shape[2] // (streams * rows)
    features = jnp.transpose(
        layer_input[0].reshape(SPAN, per_tensor, streams, rows), (2, 0, 1, 3)
    ).reshape(streams, SPAN, per_tensor * rows)
    features = lax.all_gather(swap(features, "dp"), "tensor", axis=0)
    features = features.reshape(tensors, streams * SPAN, per_tensor * rows)

    dxp, dc, db, dcum = call(
        intra_kernel,
        [shaped((SPAN, width), f32), tile, tile, tile],
        cum,
        x,
        dy,
        b,
        c,
        skip_gain[None],
        scratch=[pltpu.VMEM((SPAN, SPAN), f32)],
        flops=20 * SPAN * SPAN * width,
    )
    state = shaped((seqs, N, piece), bf16)
    starts, ends = call(scan_kernel, [state, state], got, flops=8 * N * width)
    starts = swap(starts, "seq")
    ends = swap(ends, "seq")
    grad_c, copies = call(
        grad_c_kernel,
        [shaped((SPAN, N), bf16), shaped((streams, SPAN, N), bf16)],
        dc,
        dye,
        starts,
        flops=2 * SPAN * N * width,
    )
    all_c = swap(copies, "dp").reshape(streams * SPAN, N)
    partial = lax.dot_general(
        features, all_c, (((1,), (0,)), ((), ())), preferred_element_type=f32
    ).astype(bf16)
    parts = swap(partial.reshape(seqs, rows, N), "seq")
    grad_x, grad_b, small = call(
        rest_kernel,
        [shaped((SPAN, width), bf16), shaped((SPAN, N), bf16), shaped((8, 128), f32)],
        starts,
        ends,
        x,
        dy,
        xt,
        dye,
        cum,
        loga,
        onehot,
        b,
        c,
        dxp,
        db,
        dcum,
        flops=6 * SPAN * N * width,
    )
    shard, sums = call(
        shard_kernel,
        [shaped((rows, N), f32), shaped((seqs, 8, 128), f32)],
        parts,
        small,
        flops=seqs * rows * N,
    )
    sums = jnp.sum(swap(sums, "seq"), axis=0)
    sums = jnp.sum(swap(jnp.broadcast_to(sums[None], (streams, 8, 128)), "dp"), axis=0)
    squares = jnp.broadcast_to(sums[None], (tensors, 8, 128))
    square_total = jnp.sum(swap(squares, "tensor")[:, 0, 127])
    levels = decay_rate.shape[1]
    grad_lograte = sums[:levels, :heads].T
    grad_skip = sums[0, heads : 2 * heads]

    dim = weight_c.shape[0] * seqs * streams * weight_c.shape[1] * tensors
    limit = 0.25 * math.sqrt(dim)
    clipped = shard * (limit / jnp.maximum(jnp.sqrt(square_total), limit))
    new_moment = beta_one * moment_one + (1.0 - beta_one) * clipped
    new_second = beta_two * moment_two + (1.0 - beta_two) * clipped * clipped
    direction = (
        new_moment
        / (1.0 - beta_one**step_count)
        / (jnp.sqrt(new_second / (1.0 - beta_two**step_count)) + adam_eps)
    )
    new_weight = weight_c - learn_rate * (direction + decay_weight * weight_c)
    return (
        grad_x[None],
        grad_b[None],
        grad_c[None],
        grad_lograte,
        grad_skip,
        new_weight,
        new_moment,
        new_second,
    )


def solution(mesh):
    wide = P("dp", "seq", "tensor")
    shard = P(("seq", "dp"), "tensor")
    return jax.shard_map(
        local,
        mesh=mesh,
        in_specs=(
            wide,
            wide,
            wide,
            wide,
            wide,
            P("tensor", None),
            P("tensor"),
            wide,
            wide,
            shard,
            shard,
            shard,
        ),
        out_specs=(wide, wide, wide, P("tensor", None), P("tensor"), shard, shard, shard),
        check_vma=False,
    )
```

```python
import functools
import math

import jax
import jax.numpy as jnp
from jax import lax
from jax.experimental import pallas as pl
from jax.experimental.pallas import tpu as pltpu
from jax.sharding import PartitionSpec as P

P_SIZE = 64
N = 128
SPAN = 128
PAIR = 2 * P_SIZE
LOG_ROWS = 16
GROUP = 4

beta_one = 0.9
beta_two = 0.95
adam_eps = 1e-08
learn_rate = 0.02
decay_weight = 0.1
step_count = 10

f32 = jnp.float32
bf16 = jnp.bfloat16
HIGHEST = lax.Precision.HIGHEST


def iota(shape, dim):
    return lax.broadcasted_iota(jnp.int32, shape, dim)


def dot(a, b):
    return jnp.dot(a, b, preferred_element_type=f32)


def dot_nt(a, b):
    return lax.dot_general(a, b, (((1,), (1,)), ((), ())), preferred_element_type=f32)


def first_head():
    return iota((SPAN, PAIR), 1) < P_SIZE


def spread(cols, j, first):
    return jnp.where(
        first[: cols.shape[0]], cols[:, 2 * j : 2 * j + 1], cols[:, 2 * j + 1 : 2 * j + 2]
    )


def log_rows(whole):
    row = iota((LOG_ROWS, whole.shape[1]), 0)
    high = whole.astype(bf16).astype(f32)
    middle = (whole - high).astype(bf16).astype(f32)
    low = whole - high - middle
    return jnp.where(
        row == 0, high, jnp.where(row == 1, middle, jnp.where(row == 2, low, 0.0))
    ).astype(bf16)


def row_logs(rows):
    rows = rows.astype(f32)
    return rows[0:1] + rows[1:2] + rows[2:3]


def states_kernel(dt_t, lev, rate_t, x, dy, b, c, st, loga, cum, onehot):
    heads = dt_t.shape[0]
    levels = rate_t.shape[0]
    hit = iota((levels, heads), 0) == lev[...]
    onehot[...] = jnp.zeros_like(onehot)
    onehot[:levels, :heads] = jnp.where(hit, 1.0, 0.0)
    cum[...] = jnp.zeros_like(cum)
    cum[:levels, :heads] = jnp.where(hit, rate_t[...], 0.0)
    rate = jnp.sum(cum[:levels, :], axis=0, keepdims=True)
    cum[:heads, :] = dt_t[...]
    cum[heads:, :] = jnp.zeros_like(cum[heads:, :])
    loga[...] = -rate * cum[...].T
    lower = (iota((SPAN, SPAN), 0) >= iota((SPAN, SPAN), 1)).astype(f32)
    total = jnp.dot(lower, loga[...], precision=HIGHEST, preferred_element_type=f32)
    cum[...] = total
    last = total[SPAN - 1 :, :]
    tail = jnp.exp(last - total)
    grow = jnp.exp(total)
    b_t = b[...].astype(f32).T.astype(bf16)
    c_t = c[...].astype(f32).T.astype(bf16)
    first = first_head()
    heads_piece = heads // st.shape[0]
    for j in range(heads // 2):
        piece, at = 2 * j // heads_piece, 2 * j % heads_piece * P_SIZE
        lanes = slice(j * PAIR, (j + 1) * PAIR)
        spot = slice(at, at + PAIR)
        xs = (x[:, lanes].astype(f32) * spread(tail, j, first)).astype(bf16)
        ds = (dy[:, lanes].astype(f32) * spread(grow, j, first)).astype(bf16)
        st[piece, :N, spot] = dot(b_t, xs).astype(bf16)
        st[piece, N : 2 * N, spot] = dot(c_t, ds).astype(bf16)
        st[piece, 2 * N :, spot] = log_rows(spread(last, j, first))


def group_kernel(me, got, out):
    here = me[0] // GROUP
    count = got.shape[0]
    for at in range(0, got.shape[2], PAIR):
        lanes = slice(at, at + PAIR)
        logs = [row_logs(got[k, 2 * N :, lanes]) for k in range(count)]
        decay = [jnp.exp(a) for a in logs]
        ahead = back = jnp.zeros((N, PAIR), f32)
        for k in range(count):
            ahead = decay[k] * ahead + got[k, :N, lanes].astype(f32)
        for k in reversed(range(count)):
            back = decay[k] * back + got[k, N : 2 * N, lanes].astype(f32)
        rows = log_rows(sum(logs[1:], logs[0]))
        for k in range(out.shape[0]):
            out[k, :N, lanes] = jnp.where(k > here, ahead, back).astype(bf16)
            out[k, N:, lanes] = rows


def scan_kernel(me, got, groups, out):
    here = me[0] // GROUP
    count = got.shape[0]
    for at in range(0, got.shape[2], PAIR):
        lanes = slice(at, at + PAIR)
        decay = [jnp.exp(row_logs(got[k, 2 * N :, lanes])) for k in range(count)]
        state = back = jnp.zeros((N, PAIR), f32)
        for k in range(groups.shape[0]):
            new = jnp.exp(row_logs(groups[k, N:, lanes])) * state + groups[k, :N, lanes].astype(f32)
            state = jnp.where(k < here, new, state)
        for k in reversed(range(groups.shape[0])):
            new = jnp.exp(row_logs(groups[k, N:, lanes])) * back + groups[k, :N, lanes].astype(f32)
            back = jnp.where(k > here, new, back)
        for k in range(count):
            out[k, :N, lanes] = state.astype(bf16)
            state = decay[k] * state + got[k, :N, lanes].astype(f32)
        for k in reversed(range(count)):
            out[k, N:, lanes] = back.astype(bf16)
            back = decay[k] * back + got[k, N : 2 * N, lanes].astype(f32)


def feature_kernel(rows, me, layer, *refs):
    outs, held = refs[:-1], refs[-1]
    streams = held.shape[0]
    for at in range(0, layer.shape[1], PAIR):
        turned = layer[:, at : at + PAIR].astype(f32).T.astype(bf16)
        for part in range(0, PAIR, rows):
            index = (at + part) // rows
            stream, spot = index % streams, index // streams * rows
            held[stream, spot : spot + rows, :] = turned[part : part + rows, :]
    for k, out in enumerate(outs):
        out[...] = held[me[1] ^ k]


def stack_kernel(*refs):
    for k, part in enumerate(refs[:-1]):
        refs[-1][k] = part[...]


def weight_kernel(me, all_c, *refs):
    features, out = refs[:-1], refs[-1]
    rows = out.shape[1]
    for k, block in enumerate(features):
        total = dot(block[0], all_c[me[1]])
        for j in range(1, block.shape[0]):
            total = total + dot(block[j], all_c[me[1] ^ j])
        for q in range(block.shape[1] // rows):
            out[(me[2] ^ k) * (block.shape[1] // rows) + q] = total[q * rows : (q + 1) * rows].astype(bf16)


def intra_kernel(cum, x, dy, b, c, skip, dxp, xt, dye, dc, db, dcum, rows):
    heads = skip.shape[1]
    total = cum[...]
    tail = jnp.exp(total[SPAN - 1 :, :] - total)
    grow = jnp.exp(total)
    total_t = total.T
    keep = iota((SPAN, SPAN), 1) >= iota((SPAN, SPAN), 0)
    lane = iota((SPAN, SPAN), 1)
    first = first_head()
    gain = skip[...]
    mask_a = jnp.where(first, 1.0, 0.0).astype(bf16)
    mask_b = jnp.where(first, 0.0, 1.0).astype(bf16)
    gram_t = dot_nt(b[...], c[...])
    dgram_t = jnp.zeros((SPAN, SPAN), f32)
    columns = jnp.zeros((SPAN, SPAN), f32)
    rows[...] = jnp.zeros_like(rows)
    for j in range(heads // 2):
        lanes = slice(j * PAIR, (j + 1) * PAIR)
        x_pair, dy_pair = x[:, lanes], dy[:, lanes]
        x_two = jnp.concatenate([x_pair * mask_a, x_pair * mask_b], axis=0)
        dy_two = jnp.concatenate([dy_pair * mask_a, dy_pair * mask_b], axis=0)
        dm_two = dot_nt(x_two, dy_pair)
        mixes = []
        for k in range(2):
            h = 2 * j + k
            dm = dm_two[k * SPAN : (k + 1) * SPAN]
            diff = total_t[h : h + 1, :] - total[:, h : h + 1]
            w = jnp.exp(jnp.where(keep, jnp.minimum(diff, 0.0), -1e30))
            wd = w * dm
            dgram_t = dgram_t + wd
            q = wd * gram_t
            columns = jnp.where(lane == h, jnp.sum(q, axis=1, keepdims=True), columns)
            rows[h : h + 1, :] = jnp.sum(q, axis=0, keepdims=True)
            mixes.append((w * gram_t).astype(bf16))
        dx = dot(jnp.concatenate(mixes, axis=1), dy_two)
        dy_wide = dy_pair.astype(f32)
        dxp[:, lanes] = dx + spread(gain, j, first) * dy_wide
        xt[:, lanes] = (x_pair.astype(f32) * spread(tail, j, first)).astype(bf16)
        dye[:, lanes] = (dy_wide * spread(grow, j, first)).astype(bf16)
    dcum[...] = rows[...].T - columns
    high = dgram_t.astype(bf16)
    dc[...] = dot(high.astype(f32).T.astype(bf16), b[...])
    db[...] = dot(high, c[...])


def grad_c_kernel(dc, dye, starts, grad_c, copies):
    total = dc[...]
    pieces, width = starts.shape[0], starts.shape[2]
    for j in range(pieces):
        total = total + dot_nt(dye[:, j * width : (j + 1) * width], starts[j, :N, :])
    out = total.astype(bf16)
    grad_c[...] = out
    for k in range(copies.shape[0]):
        copies[k] = out


def halves(a):
    high = a.astype(bf16)
    return high, (a - high.astype(f32)).astype(bf16)


def rest_kernel(
    states, x, dy, xt, cum, loga, onehot, b, c, dxp, db, dcum, grad_x, grad_b, small
):
    heads = x.shape[1] // P_SIZE
    pairs_piece = states.shape[2] // PAIR
    total = cum[...]
    last = total[SPAN - 1 :, :]
    tail = jnp.exp(last - total)
    grow = jnp.exp(total)
    end = jnp.exp(last)
    first = first_head()
    row = iota((SPAN, PAIR), 0)
    lane_head = iota((PAIR, 128), 0) // P_SIZE
    column = iota((PAIR, 128), 1)
    b_total = db[...]
    d_total = dcum[...]
    skips = jnp.zeros((8, 128), f32)
    for j in range(heads // 2):
        piece, at = j // pairs_piece, j % pairs_piece * PAIR
        lanes = slice(j * PAIR, (j + 1) * PAIR)
        start, stop = states[piece, :N, at : at + PAIR], states[piece, N:, at : at + PAIR]
        xs = xt[:, lanes]
        x_wide, dy_wide = x[:, lanes].astype(f32), dy[:, lanes].astype(f32)
        falling = spread(tail, j, first)
        carried = dy_wide * spread(grow, j, first) * dot(c[...], start)
        back = falling * dot(b[...], stop)
        left = x_wide * back
        grad_x[:, lanes] = (dxp[:, lanes] + back).astype(bf16)
        b_total = b_total + dot_nt(xs, stop)
        at_end = jnp.sum(left, axis=0, keepdims=True) + spread(end, j, first) * jnp.sum(
            start.astype(f32) * stop.astype(f32), axis=0, keepdims=True
        )
        moved = carried - left + jnp.where(row == SPAN - 1, at_end, 0.0)
        skip = jnp.sum(x_wide * dy_wide, axis=0, keepdims=True)
        skip = jnp.broadcast_to(skip, (8, PAIR))
        to_head = jnp.where(column == 2 * j + lane_head, 1.0, 0.0).astype(bf16)
        to_skip = jnp.where(column == heads + 2 * j + lane_head, 1.0, 0.0).astype(bf16)
        high, low = halves(moved)
        d_total = d_total + dot(high, to_head) + dot(low, to_head)
        high, low = halves(skip)
        skips = skips + dot(high, to_skip) + dot(low, to_skip)
    grad_b[...] = b_total.astype(bf16)
    upper = (iota((SPAN, SPAN), 1) >= iota((SPAN, SPAN), 0)).astype(f32)
    dlog = jnp.dot(upper, d_total, precision=HIGHEST, preferred_element_type=f32)
    rates = jnp.sum(dlog * loga[...], axis=0, keepdims=True)
    small[...] = onehot[...] * rates + jnp.where(iota((8, 128), 0) == 0, skips, 0.0)


def shard_kernel(parts, small, shard, copies):
    total = jnp.sum(parts[...].astype(f32), axis=0)
    shard[...] = total
    square = jnp.sum(total * total)
    here = (iota((8, 128), 0) == 0) & (iota((8, 128), 1) == 127)
    out = small[...] + jnp.where(here, square, 0.0)
    for k in range(copies.shape[0]):
        copies[k] = out


def sum_kernel(got, copies):
    out = jnp.sum(got[...], axis=0)
    for k in range(copies.shape[0]):
        copies[k] = out


def update_kernel(streams, size, me, got, shard, weight, moment_one, moment_two, new_w, new_m, new_s, rates, skips):
    total = jnp.sum(got[...], axis=0)
    mine = got[me[2] * streams]
    for k in range(1, streams):
        mine = mine + got[me[2] * streams + k]
    here = (iota((8, 128), 0) == 0) & (iota((8, 128), 1) == 127)
    square = jnp.sum(jnp.where(here, total, 0.0), keepdims=True)
    heads = rates.shape[1]
    rates[...] = mine[: rates.shape[0], :heads]
    skips[...] = mine[0:1, heads : 2 * heads]
    limit = 0.25 * math.sqrt(size)
    clipped = shard[...] * (limit / jnp.maximum(jnp.sqrt(square), limit))
    moment = beta_one * moment_one[...] + (1.0 - beta_one) * clipped
    second = beta_two * moment_two[...] + (1.0 - beta_two) * clipped * clipped
    direction = (
        moment
        / (1.0 - beta_one**step_count)
        / (jnp.sqrt(second / (1.0 - beta_two**step_count)) + adam_eps)
    )
    new_w[...] = weight[...] - learn_rate * (direction + decay_weight * weight[...])
    new_m[...] = moment
    new_s[...] = second


def call(kernel, out_shapes, *args, scratch=(), flops=0, limit=32):
    size = sum(math.prod(a.shape) * a.dtype.itemsize for a in (*args, *out_shapes))
    whole = pl.BlockSpec(memory_space=pltpu.VMEM)
    scalars = pl.BlockSpec(memory_space=pltpu.SMEM)
    out = pl.pallas_call(
        kernel,
        out_shape=tuple(out_shapes),
        in_specs=[scalars if a.shape == (3,) else whole for a in args],
        scratch_shapes=list(scratch),
        compiler_params=pltpu.CompilerParams(vmem_limit_bytes=limit * 1024 * 1024),
        cost_estimate=pl.CostEstimate(flops=flops, bytes_accessed=size, transcendentals=0),
    )(*args)
    return out[0] if len(out_shapes) == 1 else out


def shaped(shape, dtype):
    return jax.ShapeDtypeStruct(shape, dtype)


def swap(a, axis, groups=None):
    return lax.all_to_all(a, axis, 0, 0, tiled=True, axis_index_groups=groups)


def trade(a, axis, k):
    count = lax.axis_size(axis)
    return lax.ppermute(a, axis, [(i, i ^ k) for i in range(count)])


def local(
    seq_values,
    proj_b,
    proj_c,
    time_step,
    decay_level,
    decay_rate,
    skip_gain,
    grad_out,
    layer_input,
    weight_c,
    moment_one,
    moment_two,
):
    seqs, streams, tensors = (lax.axis_size(a) for a in ("seq", "dp", "tensor"))
    me = jnp.stack([lax.axis_index(a) for a in ("seq", "dp", "tensor")]).astype(jnp.int32)
    x, dy, b, c = seq_values[0], grad_out[0], proj_b[0], proj_c[0]
    heads = skip_gain.shape[0]
    width = heads * P_SIZE
    piece = width // GROUP
    near = [[i + k for k in range(GROUP)] for i in range(0, seqs, GROUP)]
    far = [list(range(i, seqs, GROUP)) for i in range(GROUP)]
    tile = shaped((SPAN, 128), f32)
    small_tile = shaped((8, 128), f32)
    wide = shaped((SPAN, width), bf16)
    st, loga, cum, onehot = call(
        states_kernel,
        [shaped((GROUP, 2 * N + LOG_ROWS, piece), bf16), tile, tile, small_tile],
        time_step[0].T,
        decay_level[0],
        decay_rate.T,
        x,
        dy,
        b,
        c,
        flops=4 * SPAN * N * width,
        limit=60,
    )
    layer, st = lax.optimization_barrier((layer_input[0], st))
    got = swap(st, "seq", near)

    rows = weight_c.shape[0]
    block = layer.shape[1] // streams
    pieces = call(
        functools.partial(feature_kernel, rows),
        [shaped((block, SPAN), bf16)] * streams,
        me,
        layer,
        scratch=[pltpu.VMEM((streams, block, SPAN), bf16)],
        flops=0,
    )
    pieces = [pieces] if streams == 1 else pieces
    arrived = [trade(pieces[k], "dp", k) for k in range(1, streams)]
    got, *arrived = lax.optimization_barrier((got, *arrived))
    mine = call(stack_kernel, [shaped((streams, block, SPAN), bf16)], pieces[0], *arrived)
    features = [trade(mine, "tensor", k) for k in range(1, tensors)]

    dxp, xt, dye, dc, db, dcum = call(
        intra_kernel,
        [shaped((SPAN, width), f32), wide, wide, tile, tile, tile],
        cum,
        x,
        dy,
        b,
        c,
        skip_gain[None],
        scratch=[pltpu.VMEM((SPAN, SPAN), f32)],
        flops=20 * SPAN * SPAN * width,
    )
    ahead = call(
        group_kernel,
        [shaped((seqs // GROUP, N + LOG_ROWS, piece), bf16)],
        me,
        got,
        flops=8 * N * width,
    )
    groups = swap(ahead, "seq", far)
    groups, *features = lax.optimization_barrier((groups, *features))
    features = [mine, *features]
    states = call(
        scan_kernel,
        [shaped((GROUP, 2 * N, piece), bf16)],
        me,
        got,
        groups,
        flops=8 * N * width,
    )
    states = swap(states, "seq", near)
    grad_c, copies = call(
        grad_c_kernel,
        [shaped((SPAN, N), bf16), shaped((streams, SPAN, N), bf16)],
        dc,
        dye,
        states,
        flops=2 * SPAN * N * width,
    )
    all_c = swap(copies, "dp")
    partial = call(
        weight_kernel,
        [shaped((seqs, rows, N), bf16)],
        me,
        all_c,
        *features,
        flops=2 * tensors * layer.shape[1] * SPAN * N,
    )
    parts = swap(partial, "seq")
    grad_x, grad_b, small = call(
        rest_kernel,
        [wide, shaped((SPAN, N), bf16), small_tile],
        states,
        x,
        dy,
        xt,
        cum,
        loga,
        onehot,
        b,
        c,
        dxp,
        db,
        dcum,
        flops=6 * SPAN * N * width,
    )
    shard, sums = call(
        shard_kernel,
        [shaped((rows, N), f32), shaped((seqs, 8, 128), f32)],
        parts,
        small,
        flops=seqs * rows * N,
    )
    sums = call(sum_kernel, [shaped((tensors * streams, 8, 128), f32)], swap(sums, "seq"))
    matrix = shaped((rows, N), f32)
    size = rows * seqs * streams * N * tensors
    new_weight, new_moment, new_second, rates, skips = call(
        functools.partial(update_kernel, streams, size),
        [matrix, matrix, matrix, shaped((decay_rate.shape[1], heads), f32), shaped((1, heads), f32)],
        me,
        swap(sums, ("tensor", "dp")),
        shard,
        weight_c,
        moment_one,
        moment_two,
    )
    return (
        grad_x[None],
        grad_b[None],
        grad_c[None],
        rates.T,
        skips[0],
        new_weight,
        new_moment,
        new_second,
    )


def solution(mesh):
    wide = P("dp", "seq", "tensor")
    shard = P(("seq", "dp"), "tensor")
    return jax.shard_map(
        local,
        mesh=mesh,
        in_specs=(
            wide,
            wide,
            wide,
            wide,
            wide,
            P("tensor", None),
            P("tensor"),
            wide,
            wide,
            shard,
            shard,
            shard,
        ),
        out_specs=(wide, wide, wide, P("tensor", None), P("tensor"), shard, shard, shard),
        check_vma=False,
    )
```

```python
import functools
import math

import jax
import jax.numpy as jnp
from jax import lax
from jax.experimental import pallas as pl
from jax.experimental.pallas import tpu as pltpu
from jax.sharding import PartitionSpec as P

P_SIZE = 64
N = 128
SPAN = 128
PAIR = 2 * P_SIZE
LOG_ROWS = 16
GROUP = 4

beta_one = 0.9
beta_two = 0.95
adam_eps = 1e-08
learn_rate = 0.02
decay_weight = 0.1
step_count = 10

f32 = jnp.float32
bf16 = jnp.bfloat16
HIGHEST = lax.Precision.HIGHEST


def iota(shape, dim):
    return lax.broadcasted_iota(jnp.int32, shape, dim)


def dot(a, b):
    return jnp.dot(a, b, preferred_element_type=f32)


def dot_nt(a, b):
    return lax.dot_general(a, b, (((1,), (1,)), ((), ())), preferred_element_type=f32)


def first_head():
    return iota((SPAN, PAIR), 1) < P_SIZE


def spread(cols, j, first):
    return jnp.where(
        first[: cols.shape[0]], cols[:, 2 * j : 2 * j + 1], cols[:, 2 * j + 1 : 2 * j + 2]
    )


def log_rows(whole):
    row = iota((LOG_ROWS, whole.shape[1]), 0)
    high = whole.astype(bf16).astype(f32)
    middle = (whole - high).astype(bf16).astype(f32)
    low = whole - high - middle
    return jnp.where(
        row == 0, high, jnp.where(row == 1, middle, jnp.where(row == 2, low, 0.0))
    ).astype(bf16)


def row_logs(rows):
    rows = rows.astype(f32)
    return rows[0:1] + rows[1:2] + rows[2:3]


def states_kernel(dt_t, lev, rate_t, x, dy, b, c, st, loga, cum, onehot, b_t, c_t):
    heads = dt_t.shape[0]
    levels = rate_t.shape[0]
    step = pl.program_id(0)

    @pl.when(step == 0)
    def _():
        hit = iota((levels, heads), 0) == lev[...]
        onehot[...] = jnp.zeros_like(onehot)
        onehot[:levels, :heads] = jnp.where(hit, 1.0, 0.0)
        cum[...] = jnp.zeros_like(cum)
        cum[:levels, :heads] = jnp.where(hit, rate_t[...], 0.0)
        rate = jnp.sum(cum[:levels, :], axis=0, keepdims=True)
        cum[:heads, :] = dt_t[...]
        loga[...] = -rate * cum[...].T
        lower = (iota((SPAN, SPAN), 0) >= iota((SPAN, SPAN), 1)).astype(f32)
        cum[...] = jnp.dot(lower, loga[...], precision=HIGHEST, preferred_element_type=f32)
        b_t[...] = b[...].astype(f32).T.astype(bf16)
        c_t[...] = c[...].astype(f32).T.astype(bf16)

    count = st.shape[2] // P_SIZE
    total = pltpu.roll(cum[...], (128 - step * count) % 128, 1)
    last = total[SPAN - 1 :, :]
    tail = jnp.exp(last - total)
    grow = jnp.exp(total)
    first = first_head()
    for j in range(count // 2):
        lanes = slice(j * PAIR, (j + 1) * PAIR)
        xs = (x[:, lanes].astype(f32) * spread(tail, j, first)).astype(bf16)
        ds = (dy[:, lanes].astype(f32) * spread(grow, j, first)).astype(bf16)
        st[0, :N, lanes] = dot(b_t[...], xs).astype(bf16)
        st[0, N : 2 * N, lanes] = dot(c_t[...], ds).astype(bf16)
        st[0, 2 * N :, lanes] = log_rows(spread(last, j, first))


def group_kernel(me, got, out):
    here = me[0] // GROUP
    count = got.shape[0]
    for at in range(0, got.shape[2], PAIR):
        lanes = slice(at, at + PAIR)
        logs = [row_logs(got[k, 2 * N :, lanes]) for k in range(count)]
        decay = [jnp.exp(a) for a in logs]
        ahead = back = jnp.zeros((N, PAIR), f32)
        for k in range(count):
            ahead = decay[k] * ahead + got[k, :N, lanes].astype(f32)
        for k in reversed(range(count)):
            back = decay[k] * back + got[k, N : 2 * N, lanes].astype(f32)
        rows = log_rows(sum(logs[1:], logs[0]))
        for k in range(out.shape[0]):
            out[k, :N, lanes] = jnp.where(k > here, ahead, back).astype(bf16)
            out[k, N:, lanes] = rows


def scan_kernel(me, got, groups, ahead, *refs):
    backs, held = refs[:-1], refs[-1]
    here = me[0] // GROUP
    count = got.shape[0]
    for at in range(0, got.shape[2], PAIR):
        lanes = slice(at, at + PAIR)
        decay = [jnp.exp(row_logs(got[k, 2 * N :, lanes])) for k in range(count)]
        state = back = jnp.zeros((N, PAIR), f32)
        for k in range(groups.shape[0]):
            new = jnp.exp(row_logs(groups[k, N:, lanes])) * state + groups[k, :N, lanes].astype(f32)
            state = jnp.where(k < here, new, state)
        for k in reversed(range(groups.shape[0])):
            new = jnp.exp(row_logs(groups[k, N:, lanes])) * back + groups[k, :N, lanes].astype(f32)
            back = jnp.where(k > here, new, back)
        for k in range(count):
            ahead[k, :, lanes] = state.astype(bf16)
            state = decay[k] * state + got[k, :N, lanes].astype(f32)
        for k in reversed(range(count)):
            held[k, :, lanes] = back.astype(bf16)
            back = decay[k] * back + got[k, N : 2 * N, lanes].astype(f32)
    for k, out in enumerate(backs):
        out[...] = held[(me[0] % GROUP) ^ k]


def feature_kernel(rows, me, layer, keep, send, held):
    streams = held.shape[0]
    for at in range(0, layer.shape[1], PAIR):
        turned = layer[:, at : at + PAIR].astype(f32).T.astype(bf16)
        for part in range(0, PAIR, rows):
            index = (at + part) // rows
            stream, spot = index % streams, index // streams * rows
            held[stream, spot : spot + rows, :] = turned[part : part + rows, :]
    for k in range(keep.shape[0]):
        keep[k] = held[me[1] ^ (2 * k)]
        send[k] = held[me[1] ^ (2 * k + 1)]


def pair_kernel(keep, got, *outs):
    for k, out in enumerate(outs):
        out[0] = keep[k]
        out[1] = got[k]


def stack_kernel(*refs):
    for k, part in enumerate(refs[:-1]):
        refs[-1][2 * k] = part[0]
        refs[-1][2 * k + 1] = part[1]


def weight_kernel(plan, me, all_c, *refs):
    features, out = refs[:-1], refs[-1]
    rows = out.shape[1]
    for k, blocks in plan:
        total = None
        for index, begin in blocks:
            for j in range(features[index].shape[0]):
                term = dot(features[index][j], all_c[me[1] ^ (begin + j)])
                total = term if total is None else total + term
        count = total.shape[0] // rows
        for q in range(count):
            out[(me[2] ^ k) * count + q] = total[q * rows : (q + 1) * rows].astype(bf16)


def intra_kernel(cum, x, dy, b, c, skip, dxp, xt, dye, dc, db, dcum, rows):
    heads = skip.shape[1]
    total = cum[...]
    tail = jnp.exp(total[SPAN - 1 :, :] - total)
    grow = jnp.exp(total)
    total_t = total.T
    keep = iota((SPAN, SPAN), 1) >= iota((SPAN, SPAN), 0)
    lane = iota((SPAN, SPAN), 1)
    first = first_head()
    gain = skip[...]
    mask_a = jnp.where(first, 1.0, 0.0).astype(bf16)
    mask_b = jnp.where(first, 0.0, 1.0).astype(bf16)
    gram_t = dot_nt(b[...], c[...])
    dgram_t = jnp.zeros((SPAN, SPAN), f32)
    columns = jnp.zeros((SPAN, SPAN), f32)
    rows[...] = jnp.zeros_like(rows)
    for j in range(heads // 2):
        lanes = slice(j * PAIR, (j + 1) * PAIR)
        x_pair, dy_pair = x[:, lanes], dy[:, lanes]
        x_two = jnp.concatenate([x_pair * mask_a, x_pair * mask_b], axis=0)
        dy_two = jnp.concatenate([dy_pair * mask_a, dy_pair * mask_b], axis=0)
        dm_two = dot_nt(x_two, dy_pair)
        mixes = []
        for k in range(2):
            h = 2 * j + k
            dm = dm_two[k * SPAN : (k + 1) * SPAN]
            diff = total_t[h : h + 1, :] - total[:, h : h + 1]
            w = jnp.exp(jnp.where(keep, jnp.minimum(diff, 0.0), -1e30))
            wd = w * dm
            dgram_t = dgram_t + wd
            q = wd * gram_t
            columns = jnp.where(lane == h, jnp.sum(q, axis=1, keepdims=True), columns)
            rows[h : h + 1, :] = jnp.sum(q, axis=0, keepdims=True)
            mixes.append((w * gram_t).astype(bf16))
        dx = dot(jnp.concatenate(mixes, axis=1), dy_two)
        dy_wide = dy_pair.astype(f32)
        dxp[:, lanes] = dx + spread(gain, j, first) * dy_wide
        xt[:, lanes] = (x_pair.astype(f32) * spread(tail, j, first)).astype(bf16)
        dye[:, lanes] = (dy_wide * spread(grow, j, first)).astype(bf16)
    dcum[...] = rows[...].T - columns
    high = dgram_t.astype(bf16)
    dc[...] = dot(high.astype(f32).T.astype(bf16), b[...])
    db[...] = dot(high, c[...])


def grad_c_kernel(dc, dye, starts, grad_c, copies):
    total = dc[...]
    pieces, width = starts.shape[0], starts.shape[2]
    for j in range(pieces):
        total = total + dot_nt(dye[:, j * width : (j + 1) * width], starts[j])
    out = total.astype(bf16)
    grad_c[...] = out
    for k in range(copies.shape[0]):
        copies[k] = out


def halves(a):
    high = a.astype(bf16)
    return high, (a - high.astype(f32)).astype(bf16)


def rest_kernel(
    me, starts, end_a, end_b, end_c, end_d, x, dy, xt, cum, loga, onehot, b, c, dxp, db, dcum, grad_x, grad_b, small, ends
):
    heads = x.shape[1] // P_SIZE
    pairs_piece = starts.shape[2] // PAIR
    for k, part in enumerate((end_a, end_b, end_c, end_d)):
        ends[(me[0] % GROUP) ^ k] = part[...]
    total = cum[...]
    last = total[SPAN - 1 :, :]
    tail = jnp.exp(last - total)
    grow = jnp.exp(total)
    end = jnp.exp(last)
    first = first_head()
    row = iota((SPAN, PAIR), 0)
    lane_head = iota((PAIR, 128), 0) // P_SIZE
    column = iota((PAIR, 128), 1)
    b_total = db[...]
    d_total = dcum[...]
    skips = jnp.zeros((8, 128), f32)
    for j in range(heads // 2):
        piece, at = j // pairs_piece, j % pairs_piece * PAIR
        lanes = slice(j * PAIR, (j + 1) * PAIR)
        start, stop = starts[piece, :, at : at + PAIR], ends[piece, :, at : at + PAIR]
        xs = xt[:, lanes]
        x_wide, dy_wide = x[:, lanes].astype(f32), dy[:, lanes].astype(f32)
        falling = spread(tail, j, first)
        carried = dy_wide * spread(grow, j, first) * dot(c[...], start)
        back = falling * dot(b[...], stop)
        left = x_wide * back
        grad_x[:, lanes] = (dxp[:, lanes] + back).astype(bf16)
        b_total = b_total + dot_nt(xs, stop)
        at_end = jnp.sum(left, axis=0, keepdims=True) + spread(end, j, first) * jnp.sum(
            start.astype(f32) * stop.astype(f32), axis=0, keepdims=True
        )
        moved = carried - left + jnp.where(row == SPAN - 1, at_end, 0.0)
        skip = jnp.sum(x_wide * dy_wide, axis=0, keepdims=True)
        skip = jnp.broadcast_to(skip, (8, PAIR))
        to_head = jnp.where(column == 2 * j + lane_head, 1.0, 0.0).astype(bf16)
        to_skip = jnp.where(column == heads + 2 * j + lane_head, 1.0, 0.0).astype(bf16)
        high, low = halves(moved)
        d_total = d_total + dot(high, to_head) + dot(low, to_head)
        high, low = halves(skip)
        skips = skips + dot(high, to_skip) + dot(low, to_skip)
    grad_b[...] = b_total.astype(bf16)
    upper = (iota((SPAN, SPAN), 1) >= iota((SPAN, SPAN), 0)).astype(f32)
    dlog = jnp.dot(upper, d_total, precision=HIGHEST, preferred_element_type=f32)
    rates = jnp.sum(dlog * loga[...], axis=0, keepdims=True)
    small[...] = onehot[...] * rates + jnp.where(iota((8, 128), 0) == 0, skips, 0.0)


def shard_kernel(parts, small, shard, copies):
    total = jnp.sum(parts[...].astype(f32), axis=0)
    shard[...] = total
    square = jnp.sum(total * total)
    here = (iota((8, 128), 0) == 0) & (iota((8, 128), 1) == 127)
    out = small[...] + jnp.where(here, square, 0.0)
    for k in range(copies.shape[0]):
        copies[k] = out


def sum_kernel(got, copies):
    out = jnp.sum(got[...], axis=0)
    for k in range(copies.shape[0]):
        copies[k] = out


def update_kernel(streams, size, me, got, shard, weight, moment_one, moment_two, new_w, new_m, new_s, rates, skips):
    total = jnp.sum(got[...], axis=0)
    mine = got[me[2] * streams]
    for k in range(1, streams):
        mine = mine + got[me[2] * streams + k]
    here = (iota((8, 128), 0) == 0) & (iota((8, 128), 1) == 127)
    square = jnp.sum(jnp.where(here, total, 0.0), keepdims=True)
    heads = rates.shape[1]
    rates[...] = mine[: rates.shape[0], :heads]
    skips[...] = mine[0:1, heads : 2 * heads]
    limit = 0.25 * math.sqrt(size)
    clipped = shard[...] * (limit / jnp.maximum(jnp.sqrt(square), limit))
    moment = beta_one * moment_one[...] + (1.0 - beta_one) * clipped
    second = beta_two * moment_two[...] + (1.0 - beta_two) * clipped * clipped
    direction = (
        moment
        / (1.0 - beta_one**step_count)
        / (jnp.sqrt(second / (1.0 - beta_two**step_count)) + adam_eps)
    )
    new_w[...] = weight[...] - learn_rate * (direction + decay_weight * weight[...])
    new_m[...] = moment
    new_s[...] = second


def call(kernel, out_shapes, *args, scratch=(), flops=0, limit=60, **grid):
    size = sum(math.prod(a.shape) * a.dtype.itemsize for a in (*args, *out_shapes))
    if not grid:
        whole = pl.BlockSpec(memory_space=pltpu.VMEM)
        scalars = pl.BlockSpec(memory_space=pltpu.SMEM)
        grid = {"in_specs": [scalars if a.shape == (3,) else whole for a in args]}
    out = pl.pallas_call(
        kernel,
        out_shape=tuple(out_shapes),
        scratch_shapes=list(scratch),
        compiler_params=pltpu.CompilerParams(vmem_limit_bytes=limit * 1024 * 1024),
        cost_estimate=pl.CostEstimate(flops=flops, bytes_accessed=size, transcendentals=0),
        **grid,
    )(*args)
    return out[0] if len(out_shapes) == 1 else out


def shaped(shape, dtype):
    return jax.ShapeDtypeStruct(shape, dtype)


def fixed(shape):
    return pl.BlockSpec(shape, lambda i: (0,) * len(shape))


def swap(a, axis, groups=None):
    return lax.all_to_all(a, axis, 0, 0, tiled=True, axis_index_groups=groups)


def trade(a, axis, k):
    count = lax.axis_size(axis)
    return lax.ppermute(a, axis, [(i, i ^ k) for i in range(count)])


def local(
    seq_values,
    proj_b,
    proj_c,
    time_step,
    decay_level,
    decay_rate,
    skip_gain,
    grad_out,
    layer_input,
    weight_c,
    moment_one,
    moment_two,
):
    seqs, streams, tensors = (lax.axis_size(a) for a in ("seq", "dp", "tensor"))
    me = jnp.stack([lax.axis_index(a) for a in ("seq", "dp", "tensor")]).astype(jnp.int32)
    x, dy, b, c = seq_values[0], grad_out[0], proj_b[0], proj_c[0]
    heads = skip_gain.shape[0]
    width = heads * P_SIZE
    piece = width // GROUP
    near = [[i + k for k in range(GROUP)] for i in range(0, seqs, GROUP)]
    far = [list(range(i, seqs, GROUP)) for i in range(GROUP)]
    tile = shaped((SPAN, 128), f32)
    small_tile = shaped((8, 128), f32)
    wide = shaped((SPAN, width), bf16)
    st, loga, cum, onehot = call(
        states_kernel,
        [shaped((GROUP, 2 * N + LOG_ROWS, piece), bf16), tile, tile, small_tile],
        time_step[0].T,
        decay_level[0],
        decay_rate.T,
        x,
        dy,
        b,
        c,
        scratch=[pltpu.VMEM((N, SPAN), bf16)] * 2,
        flops=4 * SPAN * N * width,
        grid=(GROUP,),
        in_specs=[
            fixed((heads, SPAN)),
            fixed((1, heads)),
            fixed(decay_rate.T.shape),
            pl.BlockSpec((SPAN, piece), lambda i: (0, i)),
            pl.BlockSpec((SPAN, piece), lambda i: (0, i)),
            fixed((SPAN, N)),
            fixed((SPAN, N)),
        ],
        out_specs=(
            pl.BlockSpec((1, 2 * N + LOG_ROWS, piece), lambda i: (i, 0, 0)),
            fixed((SPAN, 128)),
            fixed((SPAN, 128)),
            fixed((8, 128)),
        ),
    )
    layer, st = lax.optimization_barrier((layer_input[0], st))
    got = swap(st, "seq", near)

    rows = weight_c.shape[0]
    block = layer.shape[1] // streams
    half = max(streams // 2, 1)
    keep, send = call(
        functools.partial(feature_kernel, rows),
        [shaped((half, block, SPAN), bf16)] * 2,
        me,
        layer,
        scratch=[pltpu.VMEM((streams, block, SPAN), bf16)],
    )
    pairs = call(
        pair_kernel, [shaped((2, block, SPAN), bf16)] * half, keep, trade(send, "dp", 1)
    )
    pairs = [pairs] if half == 1 else pairs
    pairs = [pairs[0]] + [trade(pairs[k], "dp", 2 * k) for k in range(1, half)]
    got, *pairs = lax.optimization_barrier((got, *pairs))
    mine = call(stack_kernel, [shaped((streams, block, SPAN), bf16)], *pairs)
    left, right = trade(mine, "tensor", 1), trade(mine, "tensor", 3)

    dxp, xt, dye, dc, db, dcum = call(
        intra_kernel,
        [shaped((SPAN, width), f32), wide, wide, tile, tile, tile],
        cum,
        x,
        dy,
        b,
        c,
        skip_gain[None],
        scratch=[pltpu.VMEM((SPAN, SPAN), f32)],
        flops=20 * SPAN * SPAN * width,
    )
    ahead = call(
        group_kernel,
        [shaped((seqs // GROUP, N + LOG_ROWS, piece), bf16)],
        me,
        got,
        flops=8 * N * width,
    )
    groups = swap(ahead, "seq", far)
    groups, left, right = lax.optimization_barrier((groups, left, right))
    far_a = trade(right[:half], "tensor", 1)
    far_b = trade(left[half:], "tensor", 3)
    plan = ((0, ((0, 0),)), (1, ((1, 0),)), (3, ((2, 0),)), (2, ((3, 0), (4, half))))
    starts, *ends = call(
        scan_kernel,
        [shaped((GROUP, N, piece), bf16)] + [shaped((N, piece), bf16)] * GROUP,
        me,
        got,
        groups,
        scratch=[pltpu.VMEM((GROUP, N, piece), bf16)],
        flops=8 * N * width,
    )
    starts = swap(starts, "seq", near)
    starts, far_a, far_b = lax.optimization_barrier((starts, far_a, far_b))
    grad_c, copies = call(
        grad_c_kernel,
        [shaped((SPAN, N), bf16), shaped((streams, SPAN, N), bf16)],
        dc,
        dye,
        starts,
        flops=2 * SPAN * N * width,
    )
    copies, *ends = lax.optimization_barrier((copies, *ends))
    ends = [ends[0]] + [trade(ends[k], "seq", k) for k in range(1, GROUP)]
    all_c = swap(copies, "dp")
    partial = call(
        functools.partial(weight_kernel, plan),
        [shaped((seqs, rows, N), bf16)],
        me,
        all_c,
        mine,
        left,
        right,
        far_a,
        far_b,
        flops=2 * tensors * layer.shape[1] * SPAN * N,
    )
    parts = swap(partial, "seq")
    grad_x, grad_b, small = call(
        rest_kernel,
        [wide, shaped((SPAN, N), bf16), small_tile],
        me,
        starts,
        *ends,
        x,
        dy,
        xt,
        cum,
        loga,
        onehot,
        b,
        c,
        dxp,
        db,
        dcum,
        scratch=[pltpu.VMEM((GROUP, N, piece), bf16)],
        flops=6 * SPAN * N * width,
    )
    shard, sums = call(
        shard_kernel,
        [shaped((rows, N), f32), shaped((seqs, 8, 128), f32)],
        parts,
        small,
        flops=seqs * rows * N,
    )
    sums = call(sum_kernel, [shaped((tensors * streams, 8, 128), f32)], swap(sums, "seq"))
    matrix = shaped((rows, N), f32)
    size = rows * seqs * streams * N * tensors
    new_weight, new_moment, new_second, rates, skips = call(
        functools.partial(update_kernel, streams, size),
        [matrix, matrix, matrix, shaped((decay_rate.shape[1], heads), f32), shaped((1, heads), f32)],
        me,
        swap(sums, ("tensor", "dp")),
        shard,
        weight_c,
        moment_one,
        moment_two,
    )
    return (
        grad_x[None],
        grad_b[None],
        grad_c[None],
        rates.T,
        skips[0],
        new_weight,
        new_moment,
        new_second,
    )


def solution(mesh):
    wide = P("dp", "seq", "tensor")
    shard = P(("seq", "dp"), "tensor")
    return jax.shard_map(
        local,
        mesh=mesh,
        in_specs=(
            wide,
            wide,
            wide,
            wide,
            wide,
            P("tensor", None),
            P("tensor"),
            wide,
            wide,
            shard,
            shard,
            shard,
        ),
        out_specs=(wide, wide, wide, P("tensor", None), P("tensor"), shard, shard, shard),
        check_vma=False,
    )
```

```python
import functools
import math

import jax
import jax.numpy as jnp
from jax import lax
from jax.experimental import pallas as pl
from jax.experimental.pallas import tpu as pltpu
from jax.sharding import PartitionSpec as P

P_SIZE = 64
N = 128
SPAN = 128
PAIR = 2 * P_SIZE
LOG_ROWS = 16
GROUP = 4

beta_one = 0.9
beta_two = 0.95
adam_eps = 1e-08
learn_rate = 0.02
decay_weight = 0.1
step_count = 10

f32 = jnp.float32
bf16 = jnp.bfloat16
HIGHEST = lax.Precision.HIGHEST


def iota(shape, dim):
    return lax.broadcasted_iota(jnp.int32, shape, dim)


def dot(a, b):
    return jnp.dot(a, b, preferred_element_type=f32)


def dot_nt(a, b):
    return lax.dot_general(a, b, (((1,), (1,)), ((), ())), preferred_element_type=f32)


def first_head():
    return iota((SPAN, PAIR), 1) < P_SIZE


def spread(cols, j, first):
    return jnp.where(
        first[: cols.shape[0]], cols[:, 2 * j : 2 * j + 1], cols[:, 2 * j + 1 : 2 * j + 2]
    )


def log_rows(whole):
    row = iota((LOG_ROWS, whole.shape[1]), 0)
    high = whole.astype(bf16).astype(f32)
    middle = (whole - high).astype(bf16).astype(f32)
    low = whole - high - middle
    return jnp.where(
        row == 0, high, jnp.where(row == 1, middle, jnp.where(row == 2, low, 0.0))
    ).astype(bf16)


def row_logs(rows):
    rows = rows.astype(f32)
    return rows[0:1] + rows[1:2] + rows[2:3]


def states_kernel(dt_t, lev, rate_t, x, dy, b, c, st, loga, cum, onehot):
    heads = dt_t.shape[0]
    levels = rate_t.shape[0]
    hit = iota((levels, heads), 0) == lev[...]
    onehot[...] = jnp.zeros_like(onehot)
    onehot[:levels, :heads] = jnp.where(hit, 1.0, 0.0)
    cum[...] = jnp.zeros_like(cum)
    cum[:levels, :heads] = jnp.where(hit, rate_t[...], 0.0)
    rate = jnp.sum(cum[:levels, :], axis=0, keepdims=True)
    cum[:heads, :] = dt_t[...]
    cum[heads:, :] = jnp.zeros_like(cum[heads:, :])
    loga[...] = -rate * cum[...].T
    lower = (iota((SPAN, SPAN), 0) >= iota((SPAN, SPAN), 1)).astype(f32)
    total = jnp.dot(lower, loga[...], precision=HIGHEST, preferred_element_type=f32)
    cum[...] = total
    last = total[SPAN - 1 :, :]
    tail = jnp.exp(last - total)
    grow = jnp.exp(total)
    b_t = b[...].astype(f32).T.astype(bf16)
    c_t = c[...].astype(f32).T.astype(bf16)
    first = first_head()
    heads_piece = heads // st.shape[0]
    for j in range(heads // 2):
        piece, at = 2 * j // heads_piece, 2 * j % heads_piece * P_SIZE
        lanes = slice(j * PAIR, (j + 1) * PAIR)
        spot = slice(at, at + PAIR)
        xs = (x[:, lanes].astype(f32) * spread(tail, j, first)).astype(bf16)
        ds = (dy[:, lanes].astype(f32) * spread(grow, j, first)).astype(bf16)
        st[piece, :N, spot] = dot(b_t, xs).astype(bf16)
        st[piece, N : 2 * N, spot] = dot(c_t, ds).astype(bf16)
        st[piece, 2 * N :, spot] = log_rows(spread(last, j, first))


def group_kernel(me, got, up, down):
    here = me[0] // GROUP
    count = got.shape[0]
    for at in range(0, got.shape[2], PAIR):
        lanes = slice(at, at + PAIR)
        logs = [row_logs(got[k, 2 * N :, lanes]) for k in range(count)]
        decay = [jnp.exp(a) for a in logs]
        ahead = back = jnp.zeros((N, PAIR), f32)
        for k in range(count):
            ahead = decay[k] * ahead + got[k, :N, lanes].astype(f32)
        for k in reversed(range(count)):
            back = decay[k] * back + got[k, N : 2 * N, lanes].astype(f32)
        rows = log_rows(sum(logs[1:], logs[0]))
        up[:N, lanes] = jnp.where(here < 3, ahead, back).astype(bf16)
        up[N:, lanes] = rows
        down[:N, lanes] = jnp.where(here > 0, back, ahead).astype(bf16)
        down[N:, lanes] = rows


def scan_kernel(me, got, up, down, up_two, down_two, out):
    here = me[0] // GROUP
    count = got.shape[0]

    def pick(options, lanes):
        parts = [(k, ref[:N, lanes].astype(f32), row_logs(ref[N:, lanes])) for k, ref in options]
        _, part, log = parts[0]
        for k, other, other_log in parts[1:]:
            part = jnp.where(here == k, other, part)
            log = jnp.where(here == k, other_log, log)
        return part, jnp.exp(log)

    before = (((1, up), (2, up_two), (3, down)), ((2, up), (3, up_two)), ((3, up),))
    after = (((2, down), (1, down_two), (0, up)), ((1, down), (0, down_two)), ((0, down),))
    for at in range(0, got.shape[2], PAIR):
        lanes = slice(at, at + PAIR)
        decay = [jnp.exp(row_logs(got[k, 2 * N :, lanes])) for k in range(count)]
        state = back = jnp.zeros((N, PAIR), f32)
        for k, options in enumerate(before):
            part, fade = pick(options, lanes)
            state = jnp.where(k < here, fade * state + part, state)
        for k, options in enumerate(after):
            part, fade = pick(options, lanes)
            back = jnp.where(3 - k > here, fade * back + part, back)
        for k in range(count):
            out[k, :N, lanes] = state.astype(bf16)
            state = decay[k] * state + got[k, :N, lanes].astype(f32)
        for k in reversed(range(count)):
            out[k, N:, lanes] = back.astype(bf16)
            back = decay[k] * back + got[k, N : 2 * N, lanes].astype(f32)


def feature_kernel(rows, me, layer, keep, send, held):
    streams = held.shape[0]
    for at in range(0, layer.shape[1], PAIR):
        turned = layer[:, at : at + PAIR].astype(f32).T.astype(bf16)
        for part in range(0, PAIR, rows):
            index = (at + part) // rows
            stream, spot = index % streams, index // streams * rows
            held[stream, spot : spot + rows, :] = turned[part : part + rows, :]
    for k in range(keep.shape[0]):
        keep[k] = held[me[1] ^ (2 * k)]
        send[k] = held[me[1] ^ (2 * k + 1)]


def pair_kernel(keep, got, *outs):
    for k, out in enumerate(outs):
        out[0] = keep[k]
        out[1] = got[k]


def stack_kernel(*refs):
    for k, part in enumerate(refs[:-1]):
        refs[-1][2 * k] = part[0]
        refs[-1][2 * k + 1] = part[1]


def weight_kernel(plan, me, all_c, *refs):
    features, out = refs[:-1], refs[-1]
    rows = out.shape[1]
    for k, blocks in plan:
        total = None
        for index, begin in blocks:
            for j in range(features[index].shape[0]):
                term = dot(features[index][j], all_c[me[1] ^ (begin + j)])
                total = term if total is None else total + term
        count = total.shape[0] // rows
        for q in range(count):
            out[(me[2] ^ k) * count + q] = total[q * rows : (q + 1) * rows].astype(bf16)


def intra_kernel(cum, x, dy, b, c, skip, dxp, xt, dye, dc, db, dcum, rows):
    heads = skip.shape[1]
    total = cum[...]
    tail = jnp.exp(total[SPAN - 1 :, :] - total)
    grow = jnp.exp(total)
    total_t = total.T
    keep = iota((SPAN, SPAN), 1) >= iota((SPAN, SPAN), 0)
    lane = iota((SPAN, SPAN), 1)
    first = first_head()
    gain = skip[...]
    mask_a = jnp.where(first, 1.0, 0.0).astype(bf16)
    mask_b = jnp.where(first, 0.0, 1.0).astype(bf16)
    gram_t = dot_nt(b[...], c[...])
    dgram_t = jnp.zeros((SPAN, SPAN), f32)
    columns = jnp.zeros((SPAN, SPAN), f32)
    rows[...] = jnp.zeros_like(rows)
    for j in range(heads // 2):
        lanes = slice(j * PAIR, (j + 1) * PAIR)
        x_pair, dy_pair = x[:, lanes], dy[:, lanes]
        x_two = jnp.concatenate([x_pair * mask_a, x_pair * mask_b], axis=0)
        dy_two = jnp.concatenate([dy_pair * mask_a, dy_pair * mask_b], axis=0)
        dm_two = dot_nt(x_two, dy_pair)
        mixes = []
        for k in range(2):
            h = 2 * j + k
            dm = dm_two[k * SPAN : (k + 1) * SPAN]
            diff = total_t[h : h + 1, :] - total[:, h : h + 1]
            w = jnp.exp(jnp.where(keep, jnp.minimum(diff, 0.0), -1e30))
            wd = w * dm
            dgram_t = dgram_t + wd
            q = wd * gram_t
            columns = jnp.where(lane == h, jnp.sum(q, axis=1, keepdims=True), columns)
            rows[h : h + 1, :] = jnp.sum(q, axis=0, keepdims=True)
            mixes.append((w * gram_t).astype(bf16))
        dx = dot(jnp.concatenate(mixes, axis=1), dy_two)
        dy_wide = dy_pair.astype(f32)
        dxp[:, lanes] = dx + spread(gain, j, first) * dy_wide
        xt[:, lanes] = (x_pair.astype(f32) * spread(tail, j, first)).astype(bf16)
        dye[:, lanes] = (dy_wide * spread(grow, j, first)).astype(bf16)
    dcum[...] = rows[...].T - columns
    high = dgram_t.astype(bf16)
    dc[...] = dot(high.astype(f32).T.astype(bf16), b[...])
    db[...] = dot(high, c[...])


def grad_c_kernel(dc, dye, states, grad_c, copies):
    total = dc[...]
    pieces, width = states.shape[0], states.shape[2]
    for j in range(pieces):
        total = total + dot_nt(dye[:, j * width : (j + 1) * width], states[j, :N, :])
    out = total.astype(bf16)
    grad_c[...] = out
    for k in range(copies.shape[0]):
        copies[k] = out


def halves(a):
    high = a.astype(bf16)
    return high, (a - high.astype(f32)).astype(bf16)


def rest_kernel(
    states, x, dy, xt, cum, loga, onehot, b, c, dxp, db, dcum, grad_x, grad_b, small
):
    heads = x.shape[1] // P_SIZE
    pairs_piece = states.shape[2] // PAIR
    total = cum[...]
    last = total[SPAN - 1 :, :]
    tail = jnp.exp(last - total)
    grow = jnp.exp(total)
    end = jnp.exp(last)
    first = first_head()
    row = iota((SPAN, PAIR), 0)
    lane_head = iota((PAIR, 128), 0) // P_SIZE
    column = iota((PAIR, 128), 1)
    b_total = db[...]
    d_total = dcum[...]
    skips = jnp.zeros((8, 128), f32)
    for j in range(heads // 2):
        piece, at = j // pairs_piece, j % pairs_piece * PAIR
        lanes = slice(j * PAIR, (j + 1) * PAIR)
        start, stop = states[piece, :N, at : at + PAIR], states[piece, N:, at : at + PAIR]
        xs = xt[:, lanes]
        x_wide, dy_wide = x[:, lanes].astype(f32), dy[:, lanes].astype(f32)
        falling = spread(tail, j, first)
        carried = dy_wide * spread(grow, j, first) * dot(c[...], start)
        back = falling * dot(b[...], stop)
        left = x_wide * back
        grad_x[:, lanes] = (dxp[:, lanes] + back).astype(bf16)
        b_total = b_total + dot_nt(xs, stop)
        at_end = jnp.sum(left, axis=0, keepdims=True) + spread(end, j, first) * jnp.sum(
            start.astype(f32) * stop.astype(f32), axis=0, keepdims=True
        )
        moved = carried - left + jnp.where(row == SPAN - 1, at_end, 0.0)
        skip = jnp.sum(x_wide * dy_wide, axis=0, keepdims=True)
        skip = jnp.broadcast_to(skip, (8, PAIR))
        to_head = jnp.where(column == 2 * j + lane_head, 1.0, 0.0).astype(bf16)
        to_skip = jnp.where(column == heads + 2 * j + lane_head, 1.0, 0.0).astype(bf16)
        high, low = halves(moved)
        d_total = d_total + dot(high, to_head) + dot(low, to_head)
        high, low = halves(skip)
        skips = skips + dot(high, to_skip) + dot(low, to_skip)
    grad_b[...] = b_total.astype(bf16)
    upper = (iota((SPAN, SPAN), 1) >= iota((SPAN, SPAN), 0)).astype(f32)
    dlog = jnp.dot(upper, d_total, precision=HIGHEST, preferred_element_type=f32)
    rates = jnp.sum(dlog * loga[...], axis=0, keepdims=True)
    small[...] = onehot[...] * rates + jnp.where(iota((8, 128), 0) == 0, skips, 0.0)


def shard_kernel(parts, small, shard, copies):
    total = jnp.sum(parts[...].astype(f32), axis=0)
    shard[...] = total
    square = jnp.sum(total * total)
    here = (iota((8, 128), 0) == 0) & (iota((8, 128), 1) == 127)
    out = small[...] + jnp.where(here, square, 0.0)
    for k in range(copies.shape[0]):
        copies[k] = out


def sum_kernel(got, copies):
    out = jnp.sum(got[...], axis=0)
    for k in range(copies.shape[0]):
        copies[k] = out


def update_kernel(streams, size, me, got, shard, weight, moment_one, moment_two, new_w, new_m, new_s, rates, skips):
    total = jnp.sum(got[...], axis=0)
    mine = got[me[2] * streams]
    for k in range(1, streams):
        mine = mine + got[me[2] * streams + k]
    here = (iota((8, 128), 0) == 0) & (iota((8, 128), 1) == 127)
    square = jnp.sum(jnp.where(here, total, 0.0), keepdims=True)
    heads = rates.shape[1]
    rates[...] = mine[: rates.shape[0], :heads]
    skips[...] = mine[0:1, heads : 2 * heads]
    limit = 0.25 * math.sqrt(size)
    clipped = shard[...] * (limit / jnp.maximum(jnp.sqrt(square), limit))
    moment = beta_one * moment_one[...] + (1.0 - beta_one) * clipped
    second = beta_two * moment_two[...] + (1.0 - beta_two) * clipped * clipped
    direction = (
        moment
        / (1.0 - beta_one**step_count)
        / (jnp.sqrt(second / (1.0 - beta_two**step_count)) + adam_eps)
    )
    new_w[...] = weight[...] - learn_rate * (direction + decay_weight * weight[...])
    new_m[...] = moment
    new_s[...] = second


def call(kernel, out_shapes, *args, scratch=(), flops=0, limit=32):
    size = sum(math.prod(a.shape) * a.dtype.itemsize for a in (*args, *out_shapes))
    whole = pl.BlockSpec(memory_space=pltpu.VMEM)
    scalars = pl.BlockSpec(memory_space=pltpu.SMEM)
    out = pl.pallas_call(
        kernel,
        out_shape=tuple(out_shapes),
        in_specs=[scalars if a.shape == (3,) else whole for a in args],
        scratch_shapes=list(scratch),
        compiler_params=pltpu.CompilerParams(vmem_limit_bytes=limit * 1024 * 1024),
        cost_estimate=pl.CostEstimate(flops=flops, bytes_accessed=size, transcendentals=0),
    )(*args)
    return out[0] if len(out_shapes) == 1 else out


def shift(a, senders, step):
    count = lax.axis_size("seq")
    return lax.ppermute(a, "seq", [(i, (i + step) % count) for i in senders])


def shaped(shape, dtype):
    return jax.ShapeDtypeStruct(shape, dtype)


def swap(a, axis, groups=None):
    return lax.all_to_all(a, axis, 0, 0, tiled=True, axis_index_groups=groups)


def trade(a, axis, k):
    count = lax.axis_size(axis)
    return lax.ppermute(a, axis, [(i, i ^ k) for i in range(count)])


def local(
    seq_values,
    proj_b,
    proj_c,
    time_step,
    decay_level,
    decay_rate,
    skip_gain,
    grad_out,
    layer_input,
    weight_c,
    moment_one,
    moment_two,
):
    seqs, streams, tensors = (lax.axis_size(a) for a in ("seq", "dp", "tensor"))
    me = jnp.stack([lax.axis_index(a) for a in ("seq", "dp", "tensor")]).astype(jnp.int32)
    x, dy, b, c = seq_values[0], grad_out[0], proj_b[0], proj_c[0]
    heads = skip_gain.shape[0]
    width = heads * P_SIZE
    piece = width // GROUP
    near = [[i + k for k in range(GROUP)] for i in range(0, seqs, GROUP)]
    tile = shaped((SPAN, 128), f32)
    small_tile = shaped((8, 128), f32)
    wide = shaped((SPAN, width), bf16)
    st, loga, cum, onehot = call(
        states_kernel,
        [shaped((GROUP, 2 * N + LOG_ROWS, piece), bf16), tile, tile, small_tile],
        time_step[0].T,
        decay_level[0],
        decay_rate.T,
        x,
        dy,
        b,
        c,
        flops=4 * SPAN * N * width,
        limit=60,
    )
    layer, st = lax.optimization_barrier((layer_input[0], st))
    got = swap(st, "seq", near)

    rows = weight_c.shape[0]
    block = layer.shape[1] // streams
    half = max(streams // 2, 1)
    keep, send = call(
        functools.partial(feature_kernel, rows),
        [shaped((half, block, SPAN), bf16)] * 2,
        me,
        layer,
        scratch=[pltpu.VMEM((streams, block, SPAN), bf16)],
    )
    pairs = call(
        pair_kernel, [shaped((2, block, SPAN), bf16)] * half, keep, trade(send, "dp", 1)
    )
    pairs = [pairs] if half == 1 else pairs
    pairs = [pairs[0]] + [trade(pairs[k], "dp", 2 * k) for k in range(1, half)]
    got, *pairs = lax.optimization_barrier((got, *pairs))

    dxp, xt, dye, dc, db, dcum = call(
        intra_kernel,
        [shaped((SPAN, width), f32), wide, wide, tile, tile, tile],
        cum,
        x,
        dy,
        b,
        c,
        skip_gain[None],
        scratch=[pltpu.VMEM((SPAN, SPAN), f32)],
        flops=20 * SPAN * SPAN * width,
    )
    up, down = call(
        group_kernel,
        [shaped((N + LOG_ROWS, piece), bf16)] * 2,
        me,
        got,
        flops=8 * N * width,
    )
    up, down = shift(up, range(seqs), GROUP), shift(down, range(seqs), -GROUP)
    inner = range(GROUP, seqs - GROUP)
    up_two, down_two = shift(up, inner, GROUP), shift(down, inner, -GROUP)
    up_two, down_two, dye = lax.optimization_barrier((up_two, down_two, dye))
    plan = ((0, ((0, 0),)), (1, ((1, 0),)), (3, ((2, 0),)), (2, ((3, 0), (4, half))))
    states = call(
        scan_kernel,
        [shaped((GROUP, 2 * N, piece), bf16)],
        me,
        got,
        up,
        down,
        up_two,
        down_two,
        flops=8 * N * width,
    )
    states, *pairs = lax.optimization_barrier((states, *pairs))
    mine = call(stack_kernel, [shaped((streams, block, SPAN), bf16)], *pairs)
    left, right = trade(mine, "tensor", 1), trade(mine, "tensor", 3)
    far_a = trade(right[:half], "tensor", 1)
    far_b = trade(left[half:], "tensor", 3)
    states = swap(states, "seq", near)
    grad_c, copies = call(
        grad_c_kernel,
        [shaped((SPAN, N), bf16), shaped((streams, SPAN, N), bf16)],
        dc,
        dye,
        states,
        flops=2 * SPAN * N * width,
    )
    all_c = swap(copies, "dp")
    partial = call(
        functools.partial(weight_kernel, plan),
        [shaped((seqs, rows, N), bf16)],
        me,
        all_c,
        mine,
        left,
        right,
        far_a,
        far_b,
        flops=2 * tensors * layer.shape[1] * SPAN * N,
    )
    parts = swap(partial, "seq")
    grad_x, grad_b, small = call(
        rest_kernel,
        [wide, shaped((SPAN, N), bf16), small_tile],
        states,
        x,
        dy,
        xt,
        cum,
        loga,
        onehot,
        b,
        c,
        dxp,
        db,
        dcum,
        flops=6 * SPAN * N * width,
    )
    shard, sums = call(
        shard_kernel,
        [shaped((rows, N), f32), shaped((seqs, 8, 128), f32)],
        parts,
        small,
        flops=seqs * rows * N,
    )
    sums = call(sum_kernel, [shaped((tensors * streams, 8, 128), f32)], swap(sums, "seq"))
    matrix = shaped((rows, N), f32)
    size = rows * seqs * streams * N * tensors
    new_weight, new_moment, new_second, rates, skips = call(
        functools.partial(update_kernel, streams, size),
        [matrix, matrix, matrix, shaped((decay_rate.shape[1], heads), f32), shaped((1, heads), f32)],
        me,
        swap(sums, ("tensor", "dp")),
        shard,
        weight_c,
        moment_one,
        moment_two,
    )
    return (
        grad_x[None],
        grad_b[None],
        grad_c[None],
        rates.T,
        skips[0],
        new_weight,
        new_moment,
        new_second,
    )


def solution(mesh):
    wide = P("dp", "seq", "tensor")
    shard = P(("seq", "dp"), "tensor")
    return jax.shard_map(
        local,
        mesh=mesh,
        in_specs=(
            wide,
            wide,
            wide,
            wide,
            wide,
            P("tensor", None),
            P("tensor"),
            wide,
            wide,
            shard,
            shard,
            shard,
        ),
        out_specs=(wide, wide, wide, P("tensor", None), P("tensor"), shard, shard, shard),
        check_vma=False,
    )
```

```python
import functools
import math

import jax
import jax.numpy as jnp
from jax import lax
from jax.experimental import pallas as pl
from jax.experimental.pallas import tpu as pltpu
from jax.sharding import PartitionSpec as P

P_SIZE = 64
N = 128
SPAN = 128
PAIR = 2 * P_SIZE
LOG_ROWS = 16
GROUP = 4

beta_one = 0.9
beta_two = 0.95
adam_eps = 1e-08
learn_rate = 0.02
decay_weight = 0.1
step_count = 10

f32 = jnp.float32
bf16 = jnp.bfloat16
HIGHEST = lax.Precision.HIGHEST


def iota(shape, dim):
    return lax.broadcasted_iota(jnp.int32, shape, dim)


def dot(a, b):
    return jnp.dot(a, b, preferred_element_type=f32)


def dot_nt(a, b):
    return lax.dot_general(a, b, (((1,), (1,)), ((), ())), preferred_element_type=f32)


def first_head():
    return iota((SPAN, PAIR), 1) < P_SIZE


def spread(cols, j, first):
    return jnp.where(
        first[: cols.shape[0]], cols[:, 2 * j : 2 * j + 1], cols[:, 2 * j + 1 : 2 * j + 2]
    )


def log_rows(whole):
    row = iota((LOG_ROWS, whole.shape[1]), 0)
    high = whole.astype(bf16).astype(f32)
    middle = (whole - high).astype(bf16).astype(f32)
    low = whole - high - middle
    return jnp.where(
        row == 0, high, jnp.where(row == 1, middle, jnp.where(row == 2, low, 0.0))
    ).astype(bf16)


def row_logs(rows):
    rows = rows.astype(f32)
    return rows[0:1] + rows[1:2] + rows[2:3]


def states_kernel(dt_t, lev, rate_t, x, dy, b, c, st, loga, cum, onehot):
    heads = dt_t.shape[0]
    levels = rate_t.shape[0]
    hit = iota((levels, heads), 0) == lev[...]
    onehot[...] = jnp.zeros_like(onehot)
    onehot[:levels, :heads] = jnp.where(hit, 1.0, 0.0)
    cum[...] = jnp.zeros_like(cum)
    cum[:levels, :heads] = jnp.where(hit, rate_t[...], 0.0)
    rate = jnp.sum(cum[:levels, :], axis=0, keepdims=True)
    cum[:heads, :] = dt_t[...]
    cum[heads:, :] = jnp.zeros_like(cum[heads:, :])
    loga[...] = -rate * cum[...].T
    lower = (iota((SPAN, SPAN), 0) >= iota((SPAN, SPAN), 1)).astype(f32)
    total = jnp.dot(lower, loga[...], precision=HIGHEST, preferred_element_type=f32)
    cum[...] = total
    last = total[SPAN - 1 :, :]
    tail = jnp.exp(last - total)
    grow = jnp.exp(total)
    b_t = b[...].astype(f32).T.astype(bf16)
    c_t = c[...].astype(f32).T.astype(bf16)
    first = first_head()
    heads_piece = heads // st.shape[0]
    for j in range(heads // 2):
        piece, at = 2 * j // heads_piece, 2 * j % heads_piece * P_SIZE
        lanes = slice(j * PAIR, (j + 1) * PAIR)
        spot = slice(at, at + PAIR)
        xs = (x[:, lanes].astype(f32) * spread(tail, j, first)).astype(bf16)
        ds = (dy[:, lanes].astype(f32) * spread(grow, j, first)).astype(bf16)
        st[piece, :N, spot] = dot(b_t, xs).astype(bf16)
        st[piece, N : 2 * N, spot] = dot(c_t, ds).astype(bf16)
        st[piece, 2 * N :, spot] = log_rows(spread(last, j, first))


def group_kernel(me, got, up, down):
    here = me[0] // GROUP
    count = got.shape[0]
    for at in range(0, got.shape[2], PAIR):
        lanes = slice(at, at + PAIR)
        logs = [row_logs(got[k, 2 * N :, lanes]) for k in range(count)]
        decay = [jnp.exp(a) for a in logs]
        ahead = back = jnp.zeros((N, PAIR), f32)
        for k in range(count):
            ahead = decay[k] * ahead + got[k, :N, lanes].astype(f32)
        for k in reversed(range(count)):
            back = decay[k] * back + got[k, N : 2 * N, lanes].astype(f32)
        rows = log_rows(sum(logs[1:], logs[0]))
        up[:N, lanes] = jnp.where(here < 3, ahead, back).astype(bf16)
        up[N:, lanes] = rows
        down[:N, lanes] = jnp.where(here > 0, back, ahead).astype(bf16)
        down[N:, lanes] = rows


def scan_kernel(me, got, up, down, up_two, down_two, ahead, *refs):
    backs, held = refs[:-1], refs[-1]
    here = me[0] // GROUP
    count = got.shape[0]

    def pick(options, lanes):
        parts = [(k, ref[:N, lanes].astype(f32), row_logs(ref[N:, lanes])) for k, ref in options]
        _, part, log = parts[0]
        for k, other, other_log in parts[1:]:
            part = jnp.where(here == k, other, part)
            log = jnp.where(here == k, other_log, log)
        return part, jnp.exp(log)

    before = (((1, up), (2, up_two), (3, down)), ((2, up), (3, up_two)), ((3, up),))
    after = (((2, down), (1, down_two), (0, up)), ((1, down), (0, down_two)), ((0, down),))
    for at in range(0, got.shape[2], PAIR):
        lanes = slice(at, at + PAIR)
        decay = [jnp.exp(row_logs(got[k, 2 * N :, lanes])) for k in range(count)]
        state = back = jnp.zeros((N, PAIR), f32)
        for k, options in enumerate(before):
            part, fade = pick(options, lanes)
            state = jnp.where(k < here, fade * state + part, state)
        for k, options in enumerate(after):
            part, fade = pick(options, lanes)
            back = jnp.where(3 - k > here, fade * back + part, back)
        for k in range(count):
            ahead[k, :, lanes] = state.astype(bf16)
            state = decay[k] * state + got[k, :N, lanes].astype(f32)
        for k in reversed(range(count)):
            held[k, :, lanes] = back.astype(bf16)
            back = decay[k] * back + got[k, N : 2 * N, lanes].astype(f32)
    for k, out in enumerate(backs):
        out[...] = held[(me[0] % GROUP) ^ k]


def feature_kernel(rows, me, layer, keep, send, held):
    streams = held.shape[0]
    for at in range(0, layer.shape[1], PAIR):
        turned = layer[:, at : at + PAIR].astype(f32).T.astype(bf16)
        for part in range(0, PAIR, rows):
            index = (at + part) // rows
            stream, spot = index % streams, index // streams * rows
            held[stream, spot : spot + rows, :] = turned[part : part + rows, :]
    for k in range(keep.shape[0]):
        keep[k] = held[me[1] ^ (2 * k)]
        send[k] = held[me[1] ^ (2 * k + 1)]


def pair_kernel(keep, got, *outs):
    for k, out in enumerate(outs):
        out[0] = keep[k]
        out[1] = got[k]


def stack_kernel(*refs):
    for k, part in enumerate(refs[:-1]):
        refs[-1][2 * k] = part[0]
        refs[-1][2 * k + 1] = part[1]


def weight_kernel(plan, me, all_c, *refs):
    features, out = refs[:-1], refs[-1]
    rows = out.shape[1]
    for k, blocks in plan:
        total = None
        for index, begin in blocks:
            for j in range(features[index].shape[0]):
                term = dot(features[index][j], all_c[me[1] ^ (begin + j)])
                total = term if total is None else total + term
        count = total.shape[0] // rows
        for q in range(count):
            out[(me[2] ^ k) * count + q] = total[q * rows : (q + 1) * rows].astype(bf16)


def intra_kernel(cum, x, dy, b, c, skip, dxp, xt, dye, dc, db, dcum, rows):
    heads = skip.shape[1]
    total = cum[...]
    tail = jnp.exp(total[SPAN - 1 :, :] - total)
    grow = jnp.exp(total)
    total_t = total.T
    keep = iota((SPAN, SPAN), 1) >= iota((SPAN, SPAN), 0)
    lane = iota((SPAN, SPAN), 1)
    first = first_head()
    gain = skip[...]
    mask_a = jnp.where(first, 1.0, 0.0).astype(bf16)
    mask_b = jnp.where(first, 0.0, 1.0).astype(bf16)
    gram_t = dot_nt(b[...], c[...])
    dgram_t = jnp.zeros((SPAN, SPAN), f32)
    columns = jnp.zeros((SPAN, SPAN), f32)
    rows[...] = jnp.zeros_like(rows)
    for j in range(heads // 2):
        lanes = slice(j * PAIR, (j + 1) * PAIR)
        x_pair, dy_pair = x[:, lanes], dy[:, lanes]
        x_two = jnp.concatenate([x_pair * mask_a, x_pair * mask_b], axis=0)
        dy_two = jnp.concatenate([dy_pair * mask_a, dy_pair * mask_b], axis=0)
        dm_two = dot_nt(x_two, dy_pair)
        mixes = []
        for k in range(2):
            h = 2 * j + k
            dm = dm_two[k * SPAN : (k + 1) * SPAN]
            diff = total_t[h : h + 1, :] - total[:, h : h + 1]
            w = jnp.exp(jnp.where(keep, jnp.minimum(diff, 0.0), -1e30))
            wd = w * dm
            dgram_t = dgram_t + wd
            q = wd * gram_t
            columns = jnp.where(lane == h, jnp.sum(q, axis=1, keepdims=True), columns)
            rows[h : h + 1, :] = jnp.sum(q, axis=0, keepdims=True)
            mixes.append((w * gram_t).astype(bf16))
        dx = dot(jnp.concatenate(mixes, axis=1), dy_two)
        dy_wide = dy_pair.astype(f32)
        dxp[:, lanes] = dx + spread(gain, j, first) * dy_wide
        xt[:, lanes] = (x_pair.astype(f32) * spread(tail, j, first)).astype(bf16)
        dye[:, lanes] = (dy_wide * spread(grow, j, first)).astype(bf16)
    dcum[...] = rows[...].T - columns
    high = dgram_t.astype(bf16)
    dc[...] = dot(high.astype(f32).T.astype(bf16), b[...])
    db[...] = dot(high, c[...])


def grad_c_kernel(dc, dye, starts, grad_c, copies, held, sems):
    pieces, width = starts.shape[0], starts.shape[2]
    moves = []
    for j in range(pieces):
        lanes = slice(j * width, (j + 1) * width)
        moves.append(pltpu.make_async_copy(dye.at[:, lanes], held.at[:, lanes], sems.at[j]))
        moves[j].start()
    total = dc[...]
    for j in range(pieces):
        moves[j].wait()
        total = total + dot_nt(held[:, j * width : (j + 1) * width], starts[j])
    out = total.astype(bf16)
    grad_c[...] = out
    for k in range(copies.shape[0]):
        copies[k] = out


def halves(a):
    high = a.astype(bf16)
    return high, (a - high.astype(f32)).astype(bf16)


def rest_kernel(
    me, starts, end_a, end_b, end_c, end_d, x, dy, xt, cum, loga, onehot, b, c, dxp, db, dcum, grad_x, grad_b, small, ends
):
    heads = x.shape[1] // P_SIZE
    pairs_piece = starts.shape[2] // PAIR
    for k, part in enumerate((end_a, end_b, end_c, end_d)):
        ends[(me[0] % GROUP) ^ k] = part[...]
    total = cum[...]
    last = total[SPAN - 1 :, :]
    tail = jnp.exp(last - total)
    grow = jnp.exp(total)
    end = jnp.exp(last)
    first = first_head()
    row = iota((SPAN, PAIR), 0)
    lane_head = iota((PAIR, 128), 0) // P_SIZE
    column = iota((PAIR, 128), 1)
    b_total = db[...]
    d_total = dcum[...]
    skips = jnp.zeros((8, 128), f32)
    for j in range(heads // 2):
        piece, at = j // pairs_piece, j % pairs_piece * PAIR
        lanes = slice(j * PAIR, (j + 1) * PAIR)
        start, stop = starts[piece, :, at : at + PAIR], ends[piece, :, at : at + PAIR]
        xs = xt[:, lanes]
        x_wide, dy_wide = x[:, lanes].astype(f32), dy[:, lanes].astype(f32)
        falling = spread(tail, j, first)
        carried = dy_wide * spread(grow, j, first) * dot(c[...], start)
        back = falling * dot(b[...], stop)
        left = x_wide * back
        grad_x[:, lanes] = (dxp[:, lanes] + back).astype(bf16)
        b_total = b_total + dot_nt(xs, stop)
        at_end = jnp.sum(left, axis=0, keepdims=True) + spread(end, j, first) * jnp.sum(
            start.astype(f32) * stop.astype(f32), axis=0, keepdims=True
        )
        moved = carried - left + jnp.where(row == SPAN - 1, at_end, 0.0)
        skip = jnp.sum(x_wide * dy_wide, axis=0, keepdims=True)
        skip = jnp.broadcast_to(skip, (8, PAIR))
        to_head = jnp.where(column == 2 * j + lane_head, 1.0, 0.0).astype(bf16)
        to_skip = jnp.where(column == heads + 2 * j + lane_head, 1.0, 0.0).astype(bf16)
        high, low = halves(moved)
        d_total = d_total + dot(high, to_head) + dot(low, to_head)
        high, low = halves(skip)
        skips = skips + dot(high, to_skip) + dot(low, to_skip)
    grad_b[...] = b_total.astype(bf16)
    upper = (iota((SPAN, SPAN), 1) >= iota((SPAN, SPAN), 0)).astype(f32)
    dlog = jnp.dot(upper, d_total, precision=HIGHEST, preferred_element_type=f32)
    rates = jnp.sum(dlog * loga[...], axis=0, keepdims=True)
    small[...] = onehot[...] * rates + jnp.where(iota((8, 128), 0) == 0, skips, 0.0)


def shard_kernel(parts, small, shard, copies):
    total = jnp.sum(parts[...].astype(f32), axis=0)
    shard[...] = total
    square = jnp.sum(total * total)
    here = (iota((8, 128), 0) == 0) & (iota((8, 128), 1) == 127)
    out = small[...] + jnp.where(here, square, 0.0)
    for k in range(copies.shape[0]):
        copies[k] = out


def sum_kernel(got, copies):
    out = jnp.sum(got[...], axis=0)
    for k in range(copies.shape[0]):
        copies[k] = out


def update_kernel(streams, size, me, got, shard, weight, moment_one, moment_two, new_w, new_m, new_s, rates, skips):
    total = jnp.sum(got[...], axis=0)
    mine = got[me[2] * streams]
    for k in range(1, streams):
        mine = mine + got[me[2] * streams + k]
    here = (iota((8, 128), 0) == 0) & (iota((8, 128), 1) == 127)
    square = jnp.sum(jnp.where(here, total, 0.0), keepdims=True)
    heads = rates.shape[1]
    rates[...] = mine[: rates.shape[0], :heads]
    skips[...] = mine[0:1, heads : 2 * heads]
    limit = 0.25 * math.sqrt(size)
    clipped = shard[...] * (limit / jnp.maximum(jnp.sqrt(square), limit))
    moment = beta_one * moment_one[...] + (1.0 - beta_one) * clipped
    second = beta_two * moment_two[...] + (1.0 - beta_two) * clipped * clipped
    direction = (
        moment
        / (1.0 - beta_one**step_count)
        / (jnp.sqrt(second / (1.0 - beta_two**step_count)) + adam_eps)
    )
    new_w[...] = weight[...] - learn_rate * (direction + decay_weight * weight[...])
    new_m[...] = moment
    new_s[...] = second


def call(kernel, out_shapes, *args, scratch=(), flops=0, limit=32, hbm=(), stay=()):
    size = sum(math.prod(a.shape) * a.dtype.itemsize for a in (*args, *out_shapes))
    whole = pl.BlockSpec(memory_space=pltpu.VMEM)
    scalars = pl.BlockSpec(memory_space=pltpu.SMEM)
    far = pl.BlockSpec(memory_space=pltpu.HBM)
    count = len(out_shapes)
    args = [
        pltpu.with_memory_space_constraint(a, pltpu.HBM) if at in stay else a
        for at, a in enumerate(args)
    ]

    def body(*refs):
        ins, rest = refs[: len(args)], refs[len(args) :]
        outs, own, held = rest[:count], rest[count : count + len(scratch)], rest[count + len(scratch) :]
        shown = list(outs)
        for k, at in enumerate(hbm):
            shown[at] = held[k]
        kernel(*ins, *shown, *own)
        copies = [
            pltpu.make_async_copy(held[k], outs[at], held[-1].at[k]) for k, at in enumerate(hbm)
        ]
        for copy in copies:
            copy.start()
        for copy in copies:
            copy.wait()

    held = [pltpu.VMEM(out_shapes[at].shape, out_shapes[at].dtype) for at in hbm]
    if hbm:
        held.append(pltpu.SemaphoreType.DMA((len(hbm),)))
    out = pl.pallas_call(
        body,
        out_shape=tuple(
            pltpu.HBM(o.shape, o.dtype) if at in hbm else o for at, o in enumerate(out_shapes)
        ),
        in_specs=[
            far if at in stay else scalars if a.shape == (3,) else whole
            for at, a in enumerate(args)
        ],
        out_specs=tuple(
            far if at in hbm else whole for at in range(count)
        ),
        scratch_shapes=[*scratch, *held],
        compiler_params=pltpu.CompilerParams(vmem_limit_bytes=limit * 1024 * 1024),
        cost_estimate=pl.CostEstimate(flops=flops, bytes_accessed=size, transcendentals=0),
    )(*args)
    return out[0] if count == 1 else out


def shift(a, senders, step):
    count = lax.axis_size("seq")
    return lax.ppermute(a, "seq", [(i, (i + step) % count) for i in senders])


def shaped(shape, dtype):
    return jax.ShapeDtypeStruct(shape, dtype)


def swap(a, axis, groups=None):
    return lax.all_to_all(a, axis, 0, 0, tiled=True, axis_index_groups=groups)


def trade(a, axis, k):
    count = lax.axis_size(axis)
    return lax.ppermute(a, axis, [(i, i ^ k) for i in range(count)])


def local(
    seq_values,
    proj_b,
    proj_c,
    time_step,
    decay_level,
    decay_rate,
    skip_gain,
    grad_out,
    layer_input,
    weight_c,
    moment_one,
    moment_two,
):
    seqs, streams, tensors = (lax.axis_size(a) for a in ("seq", "dp", "tensor"))
    me = jnp.stack([lax.axis_index(a) for a in ("seq", "dp", "tensor")]).astype(jnp.int32)
    x, dy, b, c = seq_values[0], grad_out[0], proj_b[0], proj_c[0]
    heads = skip_gain.shape[0]
    width = heads * P_SIZE
    piece = width // GROUP
    near = [[i + k for k in range(GROUP)] for i in range(0, seqs, GROUP)]
    tile = shaped((SPAN, 128), f32)
    small_tile = shaped((8, 128), f32)
    wide = shaped((SPAN, width), bf16)
    st, loga, cum, onehot = call(
        states_kernel,
        [shaped((GROUP, 2 * N + LOG_ROWS, piece), bf16), tile, tile, small_tile],
        time_step[0].T,
        decay_level[0],
        decay_rate.T,
        x,
        dy,
        b,
        c,
        flops=4 * SPAN * N * width,
        limit=60,
    )
    layer, st = lax.optimization_barrier((layer_input[0], st))
    got = swap(st, "seq", near)

    rows = weight_c.shape[0]
    block = layer.shape[1] // streams
    half = max(streams // 2, 1)
    keep, send = call(
        functools.partial(feature_kernel, rows),
        [shaped((half, block, SPAN), bf16)] * 2,
        me,
        layer,
        scratch=[pltpu.VMEM((streams, block, SPAN), bf16)],
    )
    pairs = call(
        pair_kernel, [shaped((2, block, SPAN), bf16)] * half, keep, trade(send, "dp", 1)
    )
    pairs = [pairs] if half == 1 else pairs
    pairs = [pairs[0]] + [trade(pairs[k], "dp", 2 * k) for k in range(1, half)]
    got, *pairs = lax.optimization_barrier((got, *pairs))

    dxp, xt, dye, dc, db, dcum = call(
        intra_kernel,
        [shaped((SPAN, width), f32), wide, wide, tile, tile, tile],
        cum,
        x,
        dy,
        b,
        c,
        skip_gain[None],
        scratch=[pltpu.VMEM((SPAN, SPAN), f32)],
        flops=20 * SPAN * SPAN * width,
        hbm=(0, 1, 2, 4, 5),
    )
    up, down = call(
        group_kernel,
        [shaped((N + LOG_ROWS, piece), bf16)] * 2,
        me,
        got,
        flops=8 * N * width,
    )
    up, down = shift(up, range(seqs), GROUP), shift(down, range(seqs), -GROUP)
    inner = range(GROUP, seqs - GROUP)
    up_two, down_two = shift(up, inner, GROUP), shift(down, inner, -GROUP)
    up_two, down_two, dye = lax.optimization_barrier((up_two, down_two, dye))
    plan = ((0, ((0, 0),)), (1, ((1, 0),)), (3, ((2, 0),)), (2, ((3, 0), (4, half))))
    starts, *ends = call(
        scan_kernel,
        [shaped((GROUP, N, piece), bf16)] + [shaped((N, piece), bf16)] * GROUP,
        me,
        got,
        up,
        down,
        up_two,
        down_two,
        scratch=[pltpu.VMEM((GROUP, N, piece), bf16)],
        flops=8 * N * width,
        hbm=range(GROUP + 1),
    )
    starts, *pairs = lax.optimization_barrier((starts, *pairs))
    mine = call(stack_kernel, [shaped((streams, block, SPAN), bf16)], *pairs)
    left, right = trade(mine, "tensor", 1), trade(mine, "tensor", 3)
    far_a = trade(right[:half], "tensor", 1)
    far_b = trade(left[half:], "tensor", 3)
    starts = swap(starts, "seq", near)
    grad_c, copies = call(
        grad_c_kernel,
        [shaped((SPAN, N), bf16), shaped((streams, SPAN, N), bf16)],
        dc,
        dye,
        starts,
        scratch=[pltpu.VMEM((SPAN, width), bf16), pltpu.SemaphoreType.DMA((GROUP,))],
        stay=(1,),
        flops=2 * SPAN * N * width,
        hbm=(1,),
    )
    all_c = swap(copies, "dp")
    partial = call(
        functools.partial(weight_kernel, plan),
        [shaped((seqs, rows, N), bf16)],
        me,
        all_c,
        mine,
        left,
        right,
        far_a,
        far_b,
        flops=2 * tensors * layer.shape[1] * SPAN * N,
    )
    partial, *ends = lax.optimization_barrier((partial, *ends))
    parts = swap(partial, "seq")
    ends = [ends[0]] + [trade(ends[k], "seq", k) for k in range(1, GROUP)]
    grad_x, grad_b, small = call(
        rest_kernel,
        [wide, shaped((SPAN, N), bf16), small_tile],
        me,
        starts,
        *ends,
        x,
        dy,
        xt,
        cum,
        loga,
        onehot,
        b,
        c,
        dxp,
        db,
        dcum,
        scratch=[pltpu.VMEM((GROUP, N, piece), bf16)],
        flops=6 * SPAN * N * width,
    )
    shard, sums = call(
        shard_kernel,
        [shaped((rows, N), f32), shaped((seqs, 8, 128), f32)],
        parts,
        small,
        flops=seqs * rows * N,
    )
    sums = call(sum_kernel, [shaped((tensors * streams, 8, 128), f32)], swap(sums, "seq"))
    matrix = shaped((rows, N), f32)
    size = rows * seqs * streams * N * tensors
    new_weight, new_moment, new_second, rates, skips = call(
        functools.partial(update_kernel, streams, size),
        [matrix, matrix, matrix, shaped((decay_rate.shape[1], heads), f32), shaped((1, heads), f32)],
        me,
        swap(sums, ("tensor", "dp")),
        shard,
        weight_c,
        moment_one,
        moment_two,
    )
    return (
        grad_x[None],
        grad_b[None],
        grad_c[None],
        rates.T,
        skips[0],
        new_weight,
        new_moment,
        new_second,
    )


def solution(mesh):
    wide = P("dp", "seq", "tensor")
    shard = P(("seq", "dp"), "tensor")
    return jax.shard_map(
        local,
        mesh=mesh,
        in_specs=(
            wide,
            wide,
            wide,
            wide,
            wide,
            P("tensor", None),
            P("tensor"),
            wide,
            wide,
            shard,
            shard,
            shard,
        ),
        out_specs=(wide, wide, wide, P("tensor", None), P("tensor"), shard, shard, shard),
        check_vma=False,
    )
```

```python
import functools
import math

import jax
import jax.numpy as jnp
from jax import lax
from jax.experimental import pallas as pl
from jax.experimental.pallas import tpu as pltpu
from jax.sharding import Mesh
from jax.sharding import PartitionSpec as P

P_SIZE = 64
N = 128
SPAN = 128
PAIR = 2 * P_SIZE
LOG_ROWS = 16
GROUP = 4
SEQ = ("far", "near")

beta_one = 0.9
beta_two = 0.95
adam_eps = 1e-08
learn_rate = 0.02
decay_weight = 0.1
step_count = 10

f32 = jnp.float32
bf16 = jnp.bfloat16
HIGHEST = lax.Precision.HIGHEST


def iota(shape, dim):
    return lax.broadcasted_iota(jnp.int32, shape, dim)


def dot(a, b):
    return jnp.dot(a, b, preferred_element_type=f32)


def dot_nt(a, b):
    return lax.dot_general(a, b, (((1,), (1,)), ((), ())), preferred_element_type=f32)


def first_head():
    return iota((SPAN, PAIR), 1) < P_SIZE


def spread(cols, j, first):
    return jnp.where(
        first[: cols.shape[0]], cols[:, 2 * j : 2 * j + 1], cols[:, 2 * j + 1 : 2 * j + 2]
    )


def log_rows(whole):
    row = iota((LOG_ROWS, whole.shape[1]), 0)
    high = whole.astype(bf16).astype(f32)
    middle = (whole - high).astype(bf16).astype(f32)
    low = whole - high - middle
    return jnp.where(
        row == 0, high, jnp.where(row == 1, middle, jnp.where(row == 2, low, 0.0))
    ).astype(bf16)


def row_logs(rows):
    rows = rows.astype(f32)
    return rows[0:1] + rows[1:2] + rows[2:3]


def states_kernel(dt_t, lev, rate_t, x, dy, b, c, st, loga, cum, onehot):
    heads = dt_t.shape[0]
    levels = rate_t.shape[0]
    hit = iota((levels, heads), 0) == lev[...]
    onehot[...] = jnp.zeros_like(onehot)
    onehot[:levels, :heads] = jnp.where(hit, 1.0, 0.0)
    cum[...] = jnp.zeros_like(cum)
    cum[:levels, :heads] = jnp.where(hit, rate_t[...], 0.0)
    rate = jnp.sum(cum[:levels, :], axis=0, keepdims=True)
    cum[:heads, :] = dt_t[...]
    cum[heads:, :] = jnp.zeros_like(cum[heads:, :])
    loga[...] = -rate * cum[...].T
    lower = (iota((SPAN, SPAN), 0) >= iota((SPAN, SPAN), 1)).astype(f32)
    total = jnp.dot(lower, loga[...], precision=HIGHEST, preferred_element_type=f32)
    cum[...] = total
    last = total[SPAN - 1 :, :]
    tail = jnp.exp(last - total)
    grow = jnp.exp(total)
    b_t = b[...].astype(f32).T.astype(bf16)
    c_t = c[...].astype(f32).T.astype(bf16)
    first = first_head()
    heads_piece = heads // st.shape[0]
    for j in range(heads // 2):
        piece, at = 2 * j // heads_piece, 2 * j % heads_piece * P_SIZE
        lanes = slice(j * PAIR, (j + 1) * PAIR)
        spot = slice(at, at + PAIR)
        xs = (x[:, lanes].astype(f32) * spread(tail, j, first)).astype(bf16)
        ds = (dy[:, lanes].astype(f32) * spread(grow, j, first)).astype(bf16)
        st[piece, :N, spot] = dot(b_t, xs).astype(bf16)
        st[piece, N : 2 * N, spot] = dot(c_t, ds).astype(bf16)
        st[piece, 2 * N :, spot] = log_rows(spread(last, j, first))


def group_kernel(me, got, up, down):
    here = me[0] // GROUP
    count = got.shape[0]
    for at in range(0, got.shape[2], PAIR):
        lanes = slice(at, at + PAIR)
        logs = [row_logs(got[k, 2 * N :, lanes]) for k in range(count)]
        decay = [jnp.exp(a) for a in logs]
        ahead = back = jnp.zeros((N, PAIR), f32)
        for k in range(count):
            ahead = decay[k] * ahead + got[k, :N, lanes].astype(f32)
        for k in reversed(range(count)):
            back = decay[k] * back + got[k, N : 2 * N, lanes].astype(f32)
        rows = log_rows(sum(logs[1:], logs[0]))
        up[:N, lanes] = jnp.where(here < 3, ahead, back).astype(bf16)
        up[N:, lanes] = rows
        down[:N, lanes] = jnp.where(here > 0, back, ahead).astype(bf16)
        down[N:, lanes] = rows


def scan_kernel(me, got, up, down, up_two, down_two, out):
    here = me[0] // GROUP
    count = got.shape[0]

    def pick(options, lanes):
        parts = [(k, ref[:N, lanes].astype(f32), row_logs(ref[N:, lanes])) for k, ref in options]
        _, part, log = parts[0]
        for k, other, other_log in parts[1:]:
            part = jnp.where(here == k, other, part)
            log = jnp.where(here == k, other_log, log)
        return part, jnp.exp(log)

    before = (((1, up), (2, up_two), (3, down)), ((2, up), (3, up_two)), ((3, up),))
    after = (((2, down), (1, down_two), (0, up)), ((1, down), (0, down_two)), ((0, down),))
    for at in range(0, got.shape[2], PAIR):
        lanes = slice(at, at + PAIR)
        decay = [jnp.exp(row_logs(got[k, 2 * N :, lanes])) for k in range(count)]
        state = back = jnp.zeros((N, PAIR), f32)
        for k, options in enumerate(before):
            part, fade = pick(options, lanes)
            state = jnp.where(k < here, fade * state + part, state)
        for k, options in enumerate(after):
            part, fade = pick(options, lanes)
            back = jnp.where(3 - k > here, fade * back + part, back)
        for k in range(count):
            out[k, :N, lanes] = state.astype(bf16)
            state = decay[k] * state + got[k, :N, lanes].astype(f32)
        for k in reversed(range(count)):
            out[k, N:, lanes] = back.astype(bf16)
            back = decay[k] * back + got[k, N : 2 * N, lanes].astype(f32)


def feature_kernel(rows, me, layer, keep, send, held):
    streams = held.shape[0]
    for at in range(0, layer.shape[1], PAIR):
        turned = layer[:, at : at + PAIR].astype(f32).T.astype(bf16)
        for part in range(0, PAIR, rows):
            index = (at + part) // rows
            stream, spot = index % streams, index // streams * rows
            held[stream, spot : spot + rows, :] = turned[part : part + rows, :]
    for k in range(keep.shape[0]):
        keep[k] = held[me[1] ^ (2 * k)]
        send[k] = held[me[1] ^ (2 * k + 1)]


def pair_kernel(keep, got, *outs):
    for k, out in enumerate(outs):
        out[0] = keep[k]
        out[1] = got[k]


def stack_kernel(*refs):
    for k, part in enumerate(refs[:-1]):
        refs[-1][2 * k] = part[0]
        refs[-1][2 * k + 1] = part[1]


def weight_kernel(plan, me, all_c, *refs):
    features, out = refs[:-1], refs[-1]
    rows = out.shape[1]
    for k, blocks in plan:
        total = None
        for index, begin in blocks:
            for j in range(features[index].shape[0]):
                term = dot(features[index][j], all_c[me[1] ^ (begin + j)])
                total = term if total is None else total + term
        count = total.shape[0] // rows
        for q in range(count):
            out[(me[2] ^ k) * count + q] = total[q * rows : (q + 1) * rows].astype(bf16)


def intra_kernel(cum, x, dy, b, c, skip, dxp, xt, dye, dc, db, dcum, rows):
    heads = skip.shape[1]
    total = cum[...]
    tail = jnp.exp(total[SPAN - 1 :, :] - total)
    grow = jnp.exp(total)
    total_t = total.T
    keep = iota((SPAN, SPAN), 1) >= iota((SPAN, SPAN), 0)
    lane = iota((SPAN, SPAN), 1)
    first = first_head()
    gain = skip[...]
    mask_a = jnp.where(first, 1.0, 0.0).astype(bf16)
    mask_b = jnp.where(first, 0.0, 1.0).astype(bf16)
    gram_t = dot_nt(b[...], c[...])
    dgram_t = jnp.zeros((SPAN, SPAN), f32)
    columns = jnp.zeros((SPAN, SPAN), f32)
    rows[...] = jnp.zeros_like(rows)
    for j in range(heads // 2):
        lanes = slice(j * PAIR, (j + 1) * PAIR)
        x_pair, dy_pair = x[:, lanes], dy[:, lanes]
        x_two = jnp.concatenate([x_pair * mask_a, x_pair * mask_b], axis=0)
        dy_two = jnp.concatenate([dy_pair * mask_a, dy_pair * mask_b], axis=0)
        dm_two = dot_nt(x_two, dy_pair)
        mixes = []
        for k in range(2):
            h = 2 * j + k
            dm = dm_two[k * SPAN : (k + 1) * SPAN]
            diff = total_t[h : h + 1, :] - total[:, h : h + 1]
            w = jnp.exp(jnp.where(keep, jnp.minimum(diff, 0.0), -1e30))
            wd = w * dm
            dgram_t = dgram_t + wd
            q = wd * gram_t
            columns = jnp.where(lane == h, jnp.sum(q, axis=1, keepdims=True), columns)
            rows[h : h + 1, :] = jnp.sum(q, axis=0, keepdims=True)
            mixes.append((w * gram_t).astype(bf16))
        dx = dot(jnp.concatenate(mixes, axis=1), dy_two)
        dy_wide = dy_pair.astype(f32)
        dxp[:, lanes] = dx + spread(gain, j, first) * dy_wide
        xt[:, lanes] = (x_pair.astype(f32) * spread(tail, j, first)).astype(bf16)
        dye[:, lanes] = (dy_wide * spread(grow, j, first)).astype(bf16)
    dcum[...] = rows[...].T - columns
    high = dgram_t.astype(bf16)
    dc[...] = dot(high.astype(f32).T.astype(bf16), b[...])
    db[...] = dot(high, c[...])


def grad_c_kernel(dc, dye, states, grad_c, copies):
    total = dc[...]
    pieces, width = states.shape[0], states.shape[2]
    for j in range(pieces):
        total = total + dot_nt(dye[:, j * width : (j + 1) * width], states[j, :N, :])
    out = total.astype(bf16)
    grad_c[...] = out
    for k in range(copies.shape[0]):
        copies[k] = out


def halves(a):
    high = a.astype(bf16)
    return high, (a - high.astype(f32)).astype(bf16)


def rest_kernel(
    states, x, dy, xt, cum, loga, onehot, b, c, dxp, db, dcum, grad_x, grad_b, small
):
    heads = x.shape[1] // P_SIZE
    pairs_piece = states.shape[2] // PAIR
    total = cum[...]
    last = total[SPAN - 1 :, :]
    tail = jnp.exp(last - total)
    grow = jnp.exp(total)
    end = jnp.exp(last)
    first = first_head()
    row = iota((SPAN, PAIR), 0)
    lane_head = iota((PAIR, 128), 0) // P_SIZE
    column = iota((PAIR, 128), 1)
    b_total = db[...]
    d_total = dcum[...]
    skips = jnp.zeros((8, 128), f32)
    for j in range(heads // 2):
        piece, at = j // pairs_piece, j % pairs_piece * PAIR
        lanes = slice(j * PAIR, (j + 1) * PAIR)
        start, stop = states[piece, :N, at : at + PAIR], states[piece, N:, at : at + PAIR]
        xs = xt[:, lanes]
        x_wide, dy_wide = x[:, lanes].astype(f32), dy[:, lanes].astype(f32)
        falling = spread(tail, j, first)
        carried = dy_wide * spread(grow, j, first) * dot(c[...], start)
        back = falling * dot(b[...], stop)
        left = x_wide * back
        grad_x[:, lanes] = (dxp[:, lanes] + back).astype(bf16)
        b_total = b_total + dot_nt(xs, stop)
        at_end = jnp.sum(left, axis=0, keepdims=True) + spread(end, j, first) * jnp.sum(
            start.astype(f32) * stop.astype(f32), axis=0, keepdims=True
        )
        moved = carried - left + jnp.where(row == SPAN - 1, at_end, 0.0)
        skip = jnp.sum(x_wide * dy_wide, axis=0, keepdims=True)
        skip = jnp.broadcast_to(skip, (8, PAIR))
        to_head = jnp.where(column == 2 * j + lane_head, 1.0, 0.0).astype(bf16)
        to_skip = jnp.where(column == heads + 2 * j + lane_head, 1.0, 0.0).astype(bf16)
        high, low = halves(moved)
        d_total = d_total + dot(high, to_head) + dot(low, to_head)
        high, low = halves(skip)
        skips = skips + dot(high, to_skip) + dot(low, to_skip)
    grad_b[...] = b_total.astype(bf16)
    upper = (iota((SPAN, SPAN), 1) >= iota((SPAN, SPAN), 0)).astype(f32)
    dlog = jnp.dot(upper, d_total, precision=HIGHEST, preferred_element_type=f32)
    rates = jnp.sum(dlog * loga[...], axis=0, keepdims=True)
    small[...] = onehot[...] * rates + jnp.where(iota((8, 128), 0) == 0, skips, 0.0)


def shard_kernel(parts, small, shard, copies):
    total = jnp.sum(parts[...].astype(f32), axis=0)
    shard[...] = total
    square = jnp.sum(total * total)
    here = (iota((8, 128), 0) == 0) & (iota((8, 128), 1) == 127)
    out = small[...] + jnp.where(here, square, 0.0)
    for k in range(copies.shape[0]):
        copies[k] = out


def sum_kernel(got, copies):
    out = jnp.sum(got[...], axis=0)
    for k in range(copies.shape[0]):
        copies[k] = out


def update_kernel(fars, size, me, got, shard, weight, moment_one, moment_two, new_w, new_m, new_s, rates, skips):
    tensors = got.shape[0] // fars
    total = jnp.sum(got[...], axis=0)
    mine = got[me[2]]
    for k in range(1, fars):
        mine = mine + got[k * tensors + me[2]]
    here = (iota((8, 128), 0) == 0) & (iota((8, 128), 1) == 127)
    square = jnp.sum(jnp.where(here, total, 0.0), keepdims=True)
    heads = rates.shape[1]
    rates[...] = mine[: rates.shape[0], :heads]
    skips[...] = mine[0:1, heads : 2 * heads]
    limit = 0.25 * math.sqrt(size)
    clipped = shard[...] * (limit / jnp.maximum(jnp.sqrt(square), limit))
    moment = beta_one * moment_one[...] + (1.0 - beta_one) * clipped
    second = beta_two * moment_two[...] + (1.0 - beta_two) * clipped * clipped
    direction = (
        moment
        / (1.0 - beta_one**step_count)
        / (jnp.sqrt(second / (1.0 - beta_two**step_count)) + adam_eps)
    )
    new_w[...] = weight[...] - learn_rate * (direction + decay_weight * weight[...])
    new_m[...] = moment
    new_s[...] = second


def call(kernel, out_shapes, *args, scratch=(), flops=0, limit=32, hbm=(), stay=()):
    size = sum(math.prod(a.shape) * a.dtype.itemsize for a in (*args, *out_shapes))
    whole = pl.BlockSpec(memory_space=pltpu.VMEM)
    scalars = pl.BlockSpec(memory_space=pltpu.SMEM)
    far = pl.BlockSpec(memory_space=pltpu.HBM)
    count = len(out_shapes)
    args = [
        pltpu.with_memory_space_constraint(a, pltpu.HBM) if at in stay else a
        for at, a in enumerate(args)
    ]

    def body(*refs):
        ins, rest = refs[: len(args)], refs[len(args) :]
        outs, own, held = rest[:count], rest[count : count + len(scratch)], rest[count + len(scratch) :]
        shown = list(outs)
        for k, at in enumerate(hbm):
            shown[at] = held[k]
        kernel(*ins, *shown, *own)
        copies = [
            pltpu.make_async_copy(held[k], outs[at], held[-1].at[k]) for k, at in enumerate(hbm)
        ]
        for copy in copies:
            copy.start()
        for copy in copies:
            copy.wait()

    held = [pltpu.VMEM(out_shapes[at].shape, out_shapes[at].dtype) for at in hbm]
    if hbm:
        held.append(pltpu.SemaphoreType.DMA((len(hbm),)))
    out = pl.pallas_call(
        body,
        out_shape=tuple(
            pltpu.HBM(o.shape, o.dtype) if at in hbm else o for at, o in enumerate(out_shapes)
        ),
        in_specs=[
            far if at in stay else scalars if a.shape == (3,) else whole
            for at, a in enumerate(args)
        ],
        out_specs=tuple(
            far if at in hbm else whole for at in range(count)
        ),
        scratch_shapes=[*scratch, *held],
        compiler_params=pltpu.CompilerParams(vmem_limit_bytes=limit * 1024 * 1024),
        cost_estimate=pl.CostEstimate(flops=flops, bytes_accessed=size, transcendentals=0),
    )(*args)
    return out[0] if count == 1 else out


def shift(a, senders, step):
    count = lax.axis_size(SEQ)
    return lax.ppermute(a, SEQ, [(i, (i + step) % count) for i in senders])


def shaped(shape, dtype):
    return jax.ShapeDtypeStruct(shape, dtype)


def swap(a, axis):
    return lax.all_to_all(a, axis, 0, 0, tiled=True)


def trade(a, axis, k):
    count = lax.axis_size(axis)
    return lax.ppermute(a, axis, [(i, i ^ k) for i in range(count)])


def local(
    seq_values,
    proj_b,
    proj_c,
    time_step,
    decay_level,
    decay_rate,
    skip_gain,
    grad_out,
    layer_input,
    weight_c,
    moment_one,
    moment_two,
):
    seqs, streams, tensors = (lax.axis_size(a) for a in (SEQ, "dp", "tensor"))
    me = jnp.stack([lax.axis_index(a) for a in (SEQ, "dp", "tensor")]).astype(jnp.int32)
    x, dy, b, c = seq_values[0], grad_out[0], proj_b[0], proj_c[0]
    heads = skip_gain.shape[0]
    width = heads * P_SIZE
    piece = width // GROUP
    tile = shaped((SPAN, 128), f32)
    small_tile = shaped((8, 128), f32)
    wide = shaped((SPAN, width), bf16)
    st, loga, cum, onehot = call(
        states_kernel,
        [shaped((GROUP, 2 * N + LOG_ROWS, piece), bf16), tile, tile, small_tile],
        time_step[0].T,
        decay_level[0],
        decay_rate.T,
        x,
        dy,
        b,
        c,
        flops=4 * SPAN * N * width,
        limit=60,
    )
    layer, st = lax.optimization_barrier((layer_input[0], st))
    got = swap(st, "near")

    rows = weight_c.shape[0]
    block = layer.shape[1] // streams
    half = max(streams // 2, 1)
    keep, send = call(
        functools.partial(feature_kernel, rows),
        [shaped((half, block, SPAN), bf16)] * 2,
        me,
        layer,
        scratch=[pltpu.VMEM((streams, block, SPAN), bf16)],
    )
    pairs = call(
        pair_kernel, [shaped((2, block, SPAN), bf16)] * half, keep, trade(send, "dp", 1)
    )
    pairs = [pairs] if half == 1 else pairs
    pairs = [pairs[0]] + [trade(pairs[k], "dp", 2 * k) for k in range(1, half)]
    got, *pairs = lax.optimization_barrier((got, *pairs))

    dxp, xt, dye, dc, db, dcum = call(
        intra_kernel,
        [shaped((SPAN, width), f32), wide, wide, tile, tile, tile],
        cum,
        x,
        dy,
        b,
        c,
        skip_gain[None],
        scratch=[pltpu.VMEM((SPAN, SPAN), f32)],
        flops=20 * SPAN * SPAN * width,
        hbm=(0, 1, 2, 4, 5),
    )
    up, down = call(
        group_kernel,
        [shaped((N + LOG_ROWS, piece), bf16)] * 2,
        me,
        got,
        flops=8 * N * width,
    )
    up, down = shift(up, range(seqs), GROUP), shift(down, range(seqs), -GROUP)
    inner = range(GROUP, seqs - GROUP)
    up_two, down_two = shift(up, inner, GROUP), shift(down, inner, -GROUP)
    up_two, down_two, dye = lax.optimization_barrier((up_two, down_two, dye))
    plan = ((0, ((0, 0),)), (1, ((1, 0),)), (3, ((2, 0),)), (2, ((3, 0), (4, half))))
    states = call(
        scan_kernel,
        [shaped((GROUP, 2 * N, piece), bf16)],
        me,
        got,
        up,
        down,
        up_two,
        down_two,
        flops=8 * N * width,
    )
    states, *pairs = lax.optimization_barrier((states, *pairs))
    mine = call(stack_kernel, [shaped((streams, block, SPAN), bf16)], *pairs)
    left, right = trade(mine, "tensor", 1), trade(mine, "tensor", 3)
    far_a = trade(right[:half], "tensor", 1)
    far_b = trade(left[half:], "tensor", 3)
    states = swap(states, "near")
    grad_c, copies = call(
        grad_c_kernel,
        [shaped((SPAN, N), bf16), shaped((streams, SPAN, N), bf16)],
        dc,
        dye,
        states,
        flops=2 * SPAN * N * width,
        hbm=(1,),
    )
    all_c = swap(copies, "dp")
    partial = call(
        functools.partial(weight_kernel, plan),
        [shaped((seqs, rows, N), bf16)],
        me,
        all_c,
        mine,
        left,
        right,
        far_a,
        far_b,
        flops=2 * tensors * layer.shape[1] * SPAN * N,
    )
    parts = swap(partial, SEQ)
    grad_x, grad_b, small = call(
        rest_kernel,
        [wide, shaped((SPAN, N), bf16), small_tile],
        states,
        x,
        dy,
        xt,
        cum,
        loga,
        onehot,
        b,
        c,
        dxp,
        db,
        dcum,
        flops=6 * SPAN * N * width,
    )
    shard, sums = call(
        shard_kernel,
        [shaped((rows, N), f32), shaped((GROUP * streams, 8, 128), f32)],
        parts,
        small,
        flops=seqs * rows * N,
    )
    fars = seqs // GROUP
    sums = call(sum_kernel, [shaped((fars * tensors, 8, 128), f32)], swap(sums, ("near", "dp")))
    matrix = shaped((rows, N), f32)
    size = rows * seqs * streams * N * tensors
    new_weight, new_moment, new_second, rates, skips = call(
        functools.partial(update_kernel, fars, size),
        [matrix, matrix, matrix, shaped((decay_rate.shape[1], heads), f32), shaped((1, heads), f32)],
        me,
        swap(sums, ("far", "tensor")),
        shard,
        weight_c,
        moment_one,
        moment_two,
    )
    return (
        grad_x[None],
        grad_b[None],
        grad_c[None],
        rates.T,
        skips[0],
        new_weight,
        new_moment,
        new_second,
    )


def solution(mesh):
    sizes = dict(mesh.shape)
    devices = mesh.devices.reshape(-1, GROUP, sizes["tensor"], sizes["dp"])
    mesh = Mesh(devices, (*SEQ, "tensor", "dp"))
    wide = P("dp", SEQ, "tensor")
    shard = P((*SEQ, "dp"), "tensor")
    return jax.shard_map(
        local,
        mesh=mesh,
        in_specs=(
            wide,
            wide,
            wide,
            wide,
            wide,
            P("tensor", None),
            P("tensor"),
            wide,
            wide,
            shard,
            shard,
            shard,
        ),
        out_specs=(wide, wide, wide, P("tensor", None), P("tensor"), shard, shard, shard),
        check_vma=False,
    )
```

```python
import functools
import math

import jax
import jax.numpy as jnp
from jax import lax
from jax.experimental import pallas as pl
from jax.experimental.pallas import tpu as pltpu
from jax.sharding import PartitionSpec as P

P_SIZE = 64
N = 128
SPAN = 128
PAIR = 2 * P_SIZE
LOG_ROWS = 16
GROUP = 4
PARTS = 2

beta_one = 0.9
beta_two = 0.95
adam_eps = 1e-08
learn_rate = 0.02
decay_weight = 0.1
step_count = 10

f32 = jnp.float32
bf16 = jnp.bfloat16
HIGHEST = lax.Precision.HIGHEST


def iota(shape, dim):
    return lax.broadcasted_iota(jnp.int32, shape, dim)


def dot(a, b):
    return jnp.dot(a, b, preferred_element_type=f32)


def dot_nt(a, b):
    return lax.dot_general(a, b, (((1,), (1,)), ((), ())), preferred_element_type=f32)


def first_head():
    return iota((SPAN, PAIR), 1) < P_SIZE


def spread(cols, j, first):
    return jnp.where(
        first[: cols.shape[0]], cols[:, 2 * j : 2 * j + 1], cols[:, 2 * j + 1 : 2 * j + 2]
    )


def log_rows(whole):
    row = iota((LOG_ROWS, whole.shape[1]), 0)
    high = whole.astype(bf16).astype(f32)
    middle = (whole - high).astype(bf16).astype(f32)
    low = whole - high - middle
    return jnp.where(
        row == 0, high, jnp.where(row == 1, middle, jnp.where(row == 2, low, 0.0))
    ).astype(bf16)


def row_logs(rows):
    rows = rows.astype(f32)
    return rows[0:1] + rows[1:2] + rows[2:3]


def states_kernel(dt_t, lev, rate_t, x, dy, b, c, st, loga, cum, onehot):
    heads = dt_t.shape[0]
    levels = rate_t.shape[0]
    hit = iota((levels, heads), 0) == lev[...]
    onehot[...] = jnp.zeros_like(onehot)
    onehot[:levels, :heads] = jnp.where(hit, 1.0, 0.0)
    cum[...] = jnp.zeros_like(cum)
    cum[:levels, :heads] = jnp.where(hit, rate_t[...], 0.0)
    rate = jnp.sum(cum[:levels, :], axis=0, keepdims=True)
    cum[:heads, :] = dt_t[...]
    cum[heads:, :] = jnp.zeros_like(cum[heads:, :])
    loga[...] = -rate * cum[...].T
    lower = (iota((SPAN, SPAN), 0) >= iota((SPAN, SPAN), 1)).astype(f32)
    total = jnp.dot(lower, loga[...], precision=HIGHEST, preferred_element_type=f32)
    cum[...] = total
    last = total[SPAN - 1 :, :]
    tail = jnp.exp(last - total)
    grow = jnp.exp(total)
    b_t = b[...].astype(f32).T.astype(bf16)
    c_t = c[...].astype(f32).T.astype(bf16)
    first = first_head()
    heads_piece = heads // st.shape[0]
    for j in range(heads // 2):
        piece, at = 2 * j // heads_piece, 2 * j % heads_piece * P_SIZE
        lanes = slice(j * PAIR, (j + 1) * PAIR)
        spot = slice(at, at + PAIR)
        xs = (x[:, lanes].astype(f32) * spread(tail, j, first)).astype(bf16)
        ds = (dy[:, lanes].astype(f32) * spread(grow, j, first)).astype(bf16)
        st[piece, :N, spot] = dot(b_t, xs).astype(bf16)
        st[piece, N : 2 * N, spot] = dot(c_t, ds).astype(bf16)
        st[piece, 2 * N :, spot] = log_rows(spread(last, j, first))


def place(at, ref):
    width = ref.shape[1]
    return at // width, slice(at % width, at % width + PAIR)


def group_kernel(me, got, *outs):
    here = me[0] // GROUP
    count = got.shape[0]
    for at in range(0, got.shape[2], PAIR):
        lanes = slice(at, at + PAIR)
        logs = [row_logs(got[k, 2 * N :, lanes]) for k in range(count)]
        decay = [jnp.exp(a) for a in logs]
        ahead = back = jnp.zeros((N, PAIR), f32)
        for k in range(count):
            ahead = decay[k] * ahead + got[k, :N, lanes].astype(f32)
        for k in reversed(range(count)):
            back = decay[k] * back + got[k, N : 2 * N, lanes].astype(f32)
        rows = log_rows(sum(logs[1:], logs[0]))
        part, spot = place(at, outs[0])
        up, down = outs[part], outs[PARTS + part]
        up[:N, spot] = jnp.where(here < 3, ahead, back).astype(bf16)
        up[N:, spot] = rows
        down[:N, spot] = jnp.where(here > 0, back, ahead).astype(bf16)
        down[N:, spot] = rows


def scan_kernel(me, got, *refs):
    moved, out = refs[:-1], refs[-1]
    up, down, up_two, down_two = (moved[k : k + PARTS] for k in range(0, 4 * PARTS, PARTS))
    here = me[0] // GROUP
    count = got.shape[0]

    def pick(options, at):
        at_part, spot = place(at, moved[0])
        parts = [
            (k, refs[at_part][:N, spot].astype(f32), row_logs(refs[at_part][N:, spot]))
            for k, refs in options
        ]
        _, part, log = parts[0]
        for k, other, other_log in parts[1:]:
            part = jnp.where(here == k, other, part)
            log = jnp.where(here == k, other_log, log)
        return part, jnp.exp(log)

    before = (((1, up), (2, up_two), (3, down)), ((2, up), (3, up_two)), ((3, up),))
    after = (((2, down), (1, down_two), (0, up)), ((1, down), (0, down_two)), ((0, down),))
    for at in range(0, got.shape[2], PAIR):
        lanes = slice(at, at + PAIR)
        decay = [jnp.exp(row_logs(got[k, 2 * N :, lanes])) for k in range(count)]
        state = back = jnp.zeros((N, PAIR), f32)
        for k, options in enumerate(before):
            part, fade = pick(options, at)
            state = jnp.where(k < here, fade * state + part, state)
        for k, options in enumerate(after):
            part, fade = pick(options, at)
            back = jnp.where(3 - k > here, fade * back + part, back)
        for k in range(count):
            out[k, :N, lanes] = state.astype(bf16)
            state = decay[k] * state + got[k, :N, lanes].astype(f32)
        for k in reversed(range(count)):
            out[k, N:, lanes] = back.astype(bf16)
            back = decay[k] * back + got[k, N : 2 * N, lanes].astype(f32)


def feature_kernel(rows, me, layer, keep, send, held):
    streams = held.shape[0]
    for at in range(0, layer.shape[1], PAIR):
        turned = layer[:, at : at + PAIR].astype(f32).T.astype(bf16)
        for part in range(0, PAIR, rows):
            index = (at + part) // rows
            stream, spot = index % streams, index // streams * rows
            held[stream, spot : spot + rows, :] = turned[part : part + rows, :]
    for k in range(keep.shape[0]):
        keep[k] = held[me[1] ^ (2 * k)]
        send[k] = held[me[1] ^ (2 * k + 1)]


def pair_kernel(keep, got, *outs):
    for k, out in enumerate(outs):
        out[0] = keep[k]
        out[1] = got[k]


def stack_kernel(*refs):
    for k, part in enumerate(refs[:-1]):
        refs[-1][2 * k] = part[0]
        refs[-1][2 * k + 1] = part[1]


def weight_kernel(plan, me, all_c, *refs):
    features, out = refs[:-1], refs[-1]
    rows = out.shape[1]
    for k, blocks in plan:
        total = None
        for index, begin in blocks:
            for j in range(features[index].shape[0]):
                term = dot(features[index][j], all_c[me[1] ^ (begin + j)])
                total = term if total is None else total + term
        count = total.shape[0] // rows
        for q in range(count):
            out[(me[2] ^ k) * count + q] = total[q * rows : (q + 1) * rows].astype(bf16)


def intra_kernel(cum, x, dy, b, c, skip, dxp, xt, dye, dc, db, dcum, rows):
    heads = skip.shape[1]
    total = cum[...]
    tail = jnp.exp(total[SPAN - 1 :, :] - total)
    grow = jnp.exp(total)
    total_t = total.T
    keep = iota((SPAN, SPAN), 1) >= iota((SPAN, SPAN), 0)
    lane = iota((SPAN, SPAN), 1)
    first = first_head()
    gain = skip[...]
    mask_a = jnp.where(first, 1.0, 0.0).astype(bf16)
    mask_b = jnp.where(first, 0.0, 1.0).astype(bf16)
    gram_t = dot_nt(b[...], c[...])
    dgram_t = jnp.zeros((SPAN, SPAN), f32)
    columns = jnp.zeros((SPAN, SPAN), f32)
    rows[...] = jnp.zeros_like(rows)
    for j in range(heads // 2):
        lanes = slice(j * PAIR, (j + 1) * PAIR)
        x_pair, dy_pair = x[:, lanes], dy[:, lanes]
        x_two = jnp.concatenate([x_pair * mask_a, x_pair * mask_b], axis=0)
        dy_two = jnp.concatenate([dy_pair * mask_a, dy_pair * mask_b], axis=0)
        dm_two = dot_nt(x_two, dy_pair)
        mixes = []
        for k in range(2):
            h = 2 * j + k
            dm = dm_two[k * SPAN : (k + 1) * SPAN]
            diff = total_t[h : h + 1, :] - total[:, h : h + 1]
            w = jnp.exp(jnp.where(keep, jnp.minimum(diff, 0.0), -1e30))
            wd = w * dm
            dgram_t = dgram_t + wd
            q = wd * gram_t
            columns = jnp.where(lane == h, jnp.sum(q, axis=1, keepdims=True), columns)
            rows[h : h + 1, :] = jnp.sum(q, axis=0, keepdims=True)
            mixes.append((w * gram_t).astype(bf16))
        dx = dot(jnp.concatenate(mixes, axis=1), dy_two)
        dy_wide = dy_pair.astype(f32)
        dxp[:, lanes] = dx + spread(gain, j, first) * dy_wide
        xt[:, lanes] = (x_pair.astype(f32) * spread(tail, j, first)).astype(bf16)
        dye[:, lanes] = (dy_wide * spread(grow, j, first)).astype(bf16)
    dcum[...] = rows[...].T - columns
    high = dgram_t.astype(bf16)
    dc[...] = dot(high.astype(f32).T.astype(bf16), b[...])
    db[...] = dot(high, c[...])


def grad_c_kernel(dc, dye, states, grad_c, copies):
    total = dc[...]
    pieces, width = states.shape[0], states.shape[2]
    for j in range(pieces):
        total = total + dot_nt(dye[:, j * width : (j + 1) * width], states[j, :N, :])
    out = total.astype(bf16)
    grad_c[...] = out
    for k in range(copies.shape[0]):
        copies[k] = out


def halves(a):
    high = a.astype(bf16)
    return high, (a - high.astype(f32)).astype(bf16)


def rest_kernel(
    states, x, dy, xt, cum, loga, onehot, b, c, dxp, db, dcum, grad_x, grad_b, small
):
    heads = x.shape[1] // P_SIZE
    pairs_piece = states.shape[2] // PAIR
    total = cum[...]
    last = total[SPAN - 1 :, :]
    tail = jnp.exp(last - total)
    grow = jnp.exp(total)
    end = jnp.exp(last)
    first = first_head()
    row = iota((SPAN, PAIR), 0)
    lane_head = iota((PAIR, 128), 0) // P_SIZE
    column = iota((PAIR, 128), 1)
    b_total = db[...]
    d_total = dcum[...]
    skips = jnp.zeros((8, 128), f32)
    for j in range(heads // 2):
        piece, at = j // pairs_piece, j % pairs_piece * PAIR
        lanes = slice(j * PAIR, (j + 1) * PAIR)
        start, stop = states[piece, :N, at : at + PAIR], states[piece, N:, at : at + PAIR]
        xs = xt[:, lanes]
        x_wide, dy_wide = x[:, lanes].astype(f32), dy[:, lanes].astype(f32)
        falling = spread(tail, j, first)
        carried = dy_wide * spread(grow, j, first) * dot(c[...], start)
        back = falling * dot(b[...], stop)
        left = x_wide * back
        grad_x[:, lanes] = (dxp[:, lanes] + back).astype(bf16)
        b_total = b_total + dot_nt(xs, stop)
        at_end = jnp.sum(left, axis=0, keepdims=True) + spread(end, j, first) * jnp.sum(
            start.astype(f32) * stop.astype(f32), axis=0, keepdims=True
        )
        moved = carried - left + jnp.where(row == SPAN - 1, at_end, 0.0)
        skip = jnp.sum(x_wide * dy_wide, axis=0, keepdims=True)
        skip = jnp.broadcast_to(skip, (8, PAIR))
        to_head = jnp.where(column == 2 * j + lane_head, 1.0, 0.0).astype(bf16)
        to_skip = jnp.where(column == heads + 2 * j + lane_head, 1.0, 0.0).astype(bf16)
        high, low = halves(moved)
        d_total = d_total + dot(high, to_head) + dot(low, to_head)
        high, low = halves(skip)
        skips = skips + dot(high, to_skip) + dot(low, to_skip)
    grad_b[...] = b_total.astype(bf16)
    upper = (iota((SPAN, SPAN), 1) >= iota((SPAN, SPAN), 0)).astype(f32)
    dlog = jnp.dot(upper, d_total, precision=HIGHEST, preferred_element_type=f32)
    rates = jnp.sum(dlog * loga[...], axis=0, keepdims=True)
    small[...] = onehot[...] * rates + jnp.where(iota((8, 128), 0) == 0, skips, 0.0)


def shard_kernel(parts, small, shard, copies):
    total = jnp.sum(parts[...].astype(f32), axis=0)
    shard[...] = total
    square = jnp.sum(total * total)
    here = (iota((8, 128), 0) == 0) & (iota((8, 128), 1) == 127)
    out = small[...] + jnp.where(here, square, 0.0)
    for k in range(copies.shape[0]):
        copies[k] = out


def sum_kernel(got, copies):
    out = jnp.sum(got[...], axis=0)
    for k in range(copies.shape[0]):
        copies[k] = out


def update_kernel(streams, size, me, got, shard, weight, moment_one, moment_two, new_w, new_m, new_s, rates, skips):
    total = jnp.sum(got[...], axis=0)
    mine = got[me[2] * streams]
    for k in range(1, streams):
        mine = mine + got[me[2] * streams + k]
    here = (iota((8, 128), 0) == 0) & (iota((8, 128), 1) == 127)
    square = jnp.sum(jnp.where(here, total, 0.0), keepdims=True)
    heads = rates.shape[1]
    rates[...] = mine[: rates.shape[0], :heads]
    skips[...] = mine[0:1, heads : 2 * heads]
    limit = 0.25 * math.sqrt(size)
    clipped = shard[...] * (limit / jnp.maximum(jnp.sqrt(square), limit))
    moment = beta_one * moment_one[...] + (1.0 - beta_one) * clipped
    second = beta_two * moment_two[...] + (1.0 - beta_two) * clipped * clipped
    direction = (
        moment
        / (1.0 - beta_one**step_count)
        / (jnp.sqrt(second / (1.0 - beta_two**step_count)) + adam_eps)
    )
    new_w[...] = weight[...] - learn_rate * (direction + decay_weight * weight[...])
    new_m[...] = moment
    new_s[...] = second


def call(kernel, out_shapes, *args, scratch=(), flops=0, limit=32):
    size = sum(math.prod(a.shape) * a.dtype.itemsize for a in (*args, *out_shapes))
    whole = pl.BlockSpec(memory_space=pltpu.VMEM)
    scalars = pl.BlockSpec(memory_space=pltpu.SMEM)
    out = pl.pallas_call(
        kernel,
        out_shape=tuple(out_shapes),
        in_specs=[scalars if a.shape == (3,) else whole for a in args],
        scratch_shapes=list(scratch),
        compiler_params=pltpu.CompilerParams(vmem_limit_bytes=limit * 1024 * 1024),
        cost_estimate=pl.CostEstimate(flops=flops, bytes_accessed=size, transcendentals=0),
    )(*args)
    return out[0] if len(out_shapes) == 1 else out


def shift(a, senders, step):
    count = lax.axis_size("seq")
    return lax.ppermute(a, "seq", [(i, (i + step) % count) for i in senders])


def shaped(shape, dtype):
    return jax.ShapeDtypeStruct(shape, dtype)


def swap(a, axis, groups=None):
    return lax.all_to_all(a, axis, 0, 0, tiled=True, axis_index_groups=groups)


def trade(a, axis, k):
    count = lax.axis_size(axis)
    return lax.ppermute(a, axis, [(i, i ^ k) for i in range(count)])


def local(
    seq_values,
    proj_b,
    proj_c,
    time_step,
    decay_level,
    decay_rate,
    skip_gain,
    grad_out,
    layer_input,
    weight_c,
    moment_one,
    moment_two,
):
    seqs, streams, tensors = (lax.axis_size(a) for a in ("seq", "dp", "tensor"))
    me = jnp.stack([lax.axis_index(a) for a in ("seq", "dp", "tensor")]).astype(jnp.int32)
    x, dy, b, c = seq_values[0], grad_out[0], proj_b[0], proj_c[0]
    heads = skip_gain.shape[0]
    width = heads * P_SIZE
    piece = width // GROUP
    near = [[i + k for k in range(GROUP)] for i in range(0, seqs, GROUP)]
    tile = shaped((SPAN, 128), f32)
    small_tile = shaped((8, 128), f32)
    wide = shaped((SPAN, width), bf16)
    st, loga, cum, onehot = call(
        states_kernel,
        [shaped((GROUP, 2 * N + LOG_ROWS, piece), bf16), tile, tile, small_tile],
        time_step[0].T,
        decay_level[0],
        decay_rate.T,
        x,
        dy,
        b,
        c,
        flops=4 * SPAN * N * width,
        limit=60,
    )
    layer, st = lax.optimization_barrier((layer_input[0], st))
    got = swap(st, "seq", near)

    rows = weight_c.shape[0]
    block = layer.shape[1] // streams
    half = max(streams // 2, 1)
    keep, send = call(
        functools.partial(feature_kernel, rows),
        [shaped((half, block, SPAN), bf16)] * 2,
        me,
        layer,
        scratch=[pltpu.VMEM((streams, block, SPAN), bf16)],
    )
    pairs = call(
        pair_kernel, [shaped((2, block, SPAN), bf16)] * half, keep, trade(send, "dp", 1)
    )
    pairs = [pairs] if half == 1 else pairs
    pairs = [pairs[0]] + [trade(pairs[k], "dp", 2 * k) for k in range(1, half)]
    got, *pairs = lax.optimization_barrier((got, *pairs))

    dxp, xt, dye, dc, db, dcum = call(
        intra_kernel,
        [shaped((SPAN, width), f32), wide, wide, tile, tile, tile],
        cum,
        x,
        dy,
        b,
        c,
        skip_gain[None],
        scratch=[pltpu.VMEM((SPAN, SPAN), f32)],
        flops=20 * SPAN * SPAN * width,
    )
    sent = call(
        group_kernel,
        [shaped((N + LOG_ROWS, piece // PARTS), bf16)] * (2 * PARTS),
        me,
        got,
        flops=8 * N * width,
    )
    up, down = sent[:PARTS], sent[PARTS:]
    inner = range(GROUP, seqs - GROUP)
    up = [shift(a, range(seqs), GROUP) for a in up]
    down = [shift(a, range(seqs), -GROUP) for a in down]
    up_two = [shift(a, inner, GROUP) for a in up]
    down_two = [shift(a, inner, -GROUP) for a in down]
    up_two, down_two, dye = lax.optimization_barrier((up_two, down_two, dye))
    plan = ((0, ((0, 0),)), (1, ((1, 0),)), (3, ((2, 0),)), (2, ((3, 0), (4, half))))
    states = call(
        scan_kernel,
        [shaped((GROUP, 2 * N, piece), bf16)],
        me,
        got,
        *up,
        *down,
        *up_two,
        *down_two,
        flops=8 * N * width,
    )
    states, *pairs = lax.optimization_barrier((states, *pairs))
    mine = call(stack_kernel, [shaped((streams, block, SPAN), bf16)], *pairs)
    left, right = trade(mine, "tensor", 1), trade(mine, "tensor", 3)
    far_a = trade(right[:half], "tensor", 1)
    far_b = trade(left[half:], "tensor", 3)
    states = swap(states, "seq", near)
    grad_c, copies = call(
        grad_c_kernel,
        [shaped((SPAN, N), bf16), shaped((streams, SPAN, N), bf16)],
        dc,
        dye,
        states,
        flops=2 * SPAN * N * width,
    )
    all_c = swap(copies, "dp")
    partial = call(
        functools.partial(weight_kernel, plan),
        [shaped((seqs, rows, N), bf16)],
        me,
        all_c,
        mine,
        left,
        right,
        far_a,
        far_b,
        flops=2 * tensors * layer.shape[1] * SPAN * N,
    )
    parts = swap(partial, "seq")
    grad_x, grad_b, small = call(
        rest_kernel,
        [wide, shaped((SPAN, N), bf16), small_tile],
        states,
        x,
        dy,
        xt,
        cum,
        loga,
        onehot,
        b,
        c,
        dxp,
        db,
        dcum,
        flops=6 * SPAN * N * width,
    )
    shard, sums = call(
        shard_kernel,
        [shaped((rows, N), f32), shaped((seqs, 8, 128), f32)],
        parts,
        small,
        flops=seqs * rows * N,
    )
    sums = call(sum_kernel, [shaped((tensors * streams, 8, 128), f32)], swap(sums, "seq"))
    matrix = shaped((rows, N), f32)
    size = rows * seqs * streams * N * tensors
    new_weight, new_moment, new_second, rates, skips = call(
        functools.partial(update_kernel, streams, size),
        [matrix, matrix, matrix, shaped((decay_rate.shape[1], heads), f32), shaped((1, heads), f32)],
        me,
        swap(sums, ("tensor", "dp")),
        shard,
        weight_c,
        moment_one,
        moment_two,
    )
    return (
        grad_x[None],
        grad_b[None],
        grad_c[None],
        rates.T,
        skips[0],
        new_weight,
        new_moment,
        new_second,
    )


def solution(mesh):
    wide = P("dp", "seq", "tensor")
    shard = P(("seq", "dp"), "tensor")
    return jax.shard_map(
        local,
        mesh=mesh,
        in_specs=(
            wide,
            wide,
            wide,
            wide,
            wide,
            P("tensor", None),
            P("tensor"),
            wide,
            wide,
            shard,
            shard,
            shard,
        ),
        out_specs=(wide, wide, wide, P("tensor", None), P("tensor"), shard, shard, shard),
        check_vma=False,
    )
```

```python
import functools
import math

import jax
import jax.numpy as jnp
from jax import lax
from jax.experimental import pallas as pl
from jax.experimental.pallas import tpu as pltpu
from jax.sharding import PartitionSpec as P

P_SIZE = 64
N = 128
SPAN = 128
PAIR = 2 * P_SIZE
LOG_ROWS = 16
GROUP = 4

beta_one = 0.9
beta_two = 0.95
adam_eps = 1e-08
learn_rate = 0.02
decay_weight = 0.1
step_count = 10

f32 = jnp.float32
bf16 = jnp.bfloat16
HIGHEST = lax.Precision.HIGHEST


def iota(shape, dim):
    return lax.broadcasted_iota(jnp.int32, shape, dim)


def dot(a, b):
    return jnp.dot(a, b, preferred_element_type=f32)


def dot_nt(a, b):
    return lax.dot_general(a, b, (((1,), (1,)), ((), ())), preferred_element_type=f32)


def first_head():
    return iota((SPAN, PAIR), 1) < P_SIZE


def spread(cols, j, first):
    return jnp.where(
        first[: cols.shape[0]], cols[:, 2 * j : 2 * j + 1], cols[:, 2 * j + 1 : 2 * j + 2]
    )


def log_rows(whole):
    row = iota((LOG_ROWS, whole.shape[1]), 0)
    high = whole.astype(bf16).astype(f32)
    middle = (whole - high).astype(bf16).astype(f32)
    low = whole - high - middle
    return jnp.where(
        row == 0, high, jnp.where(row == 1, middle, jnp.where(row == 2, low, 0.0))
    ).astype(bf16)


def row_logs(rows):
    rows = rows.astype(f32)
    return rows[0:1] + rows[1:2] + rows[2:3]


def states_kernel(dt_t, lev, rate_t, x, dy, b, c, st, loga, cum, onehot):
    heads = dt_t.shape[0]
    levels = rate_t.shape[0]
    hit = iota((levels, heads), 0) == lev[...]
    onehot[...] = jnp.zeros_like(onehot)
    onehot[:levels, :heads] = jnp.where(hit, 1.0, 0.0)
    cum[...] = jnp.zeros_like(cum)
    cum[:levels, :heads] = jnp.where(hit, rate_t[...], 0.0)
    rate = jnp.sum(cum[:levels, :], axis=0, keepdims=True)
    cum[:heads, :] = dt_t[...]
    cum[heads:, :] = jnp.zeros_like(cum[heads:, :])
    loga[...] = -rate * cum[...].T
    lower = (iota((SPAN, SPAN), 0) >= iota((SPAN, SPAN), 1)).astype(f32)
    total = jnp.dot(lower, loga[...], precision=HIGHEST, preferred_element_type=f32)
    cum[...] = total
    last = total[SPAN - 1 :, :]
    tail = jnp.exp(last - total)
    grow = jnp.exp(total)
    b_t = b[...].astype(f32).T.astype(bf16)
    c_t = c[...].astype(f32).T.astype(bf16)
    first = first_head()
    heads_piece = heads // st.shape[0]
    for j in range(heads // 2):
        piece, at = 2 * j // heads_piece, 2 * j % heads_piece * P_SIZE
        lanes = slice(j * PAIR, (j + 1) * PAIR)
        spot = slice(at, at + PAIR)
        xs = (x[:, lanes].astype(f32) * spread(tail, j, first)).astype(bf16)
        ds = (dy[:, lanes].astype(f32) * spread(grow, j, first)).astype(bf16)
        st[piece, :N, spot] = dot(b_t, xs).astype(bf16)
        st[piece, N : 2 * N, spot] = dot(c_t, ds).astype(bf16)
        st[piece, 2 * N :, spot] = log_rows(spread(last, j, first))


def group_kernel(me, got, out):
    here = me[0] // GROUP
    count = got.shape[0]
    for at in range(0, got.shape[2], PAIR):
        lanes = slice(at, at + PAIR)
        logs = [row_logs(got[k, 2 * N :, lanes]) for k in range(count)]
        decay = [jnp.exp(a) for a in logs]
        ahead = back = jnp.zeros((N, PAIR), f32)
        for k in range(count):
            ahead = decay[k] * ahead + got[k, :N, lanes].astype(f32)
        for k in reversed(range(count)):
            back = decay[k] * back + got[k, N : 2 * N, lanes].astype(f32)
        rows = log_rows(sum(logs[1:], logs[0]))
        for k in range(out.shape[0]):
            out[k, :N, lanes] = jnp.where(k > here, ahead, back).astype(bf16)
            out[k, N:, lanes] = rows


def scan_kernel(me, got, groups, ahead, *refs):
    backs, held = refs[:-1], refs[-1]
    here = me[0] // GROUP
    count = got.shape[0]
    for at in range(0, got.shape[2], PAIR):
        lanes = slice(at, at + PAIR)
        decay = [jnp.exp(row_logs(got[k, 2 * N :, lanes])) for k in range(count)]
        state = back = jnp.zeros((N, PAIR), f32)
        for k in range(groups.shape[0]):
            new = jnp.exp(row_logs(groups[k, N:, lanes])) * state + groups[k, :N, lanes].astype(f32)
            state = jnp.where(k < here, new, state)
        for k in reversed(range(groups.shape[0])):
            new = jnp.exp(row_logs(groups[k, N:, lanes])) * back + groups[k, :N, lanes].astype(f32)
            back = jnp.where(k > here, new, back)
        for k in range(count):
            ahead[k, :, lanes] = state.astype(bf16)
            state = decay[k] * state + got[k, :N, lanes].astype(f32)
        for k in reversed(range(count)):
            held[k, :, lanes] = back.astype(bf16)
            back = decay[k] * back + got[k, N : 2 * N, lanes].astype(f32)
    for k, out in enumerate(backs):
        out[...] = held[(me[0] % GROUP) ^ k]


def feature_kernel(rows, me, layer, keep, send, held):
    streams = held.shape[0]
    for at in range(0, layer.shape[1], PAIR):
        turned = layer[:, at : at + PAIR].astype(f32).T.astype(bf16)
        for part in range(0, PAIR, rows):
            index = (at + part) // rows
            stream, spot = index % streams, index // streams * rows
            held[stream, spot : spot + rows, :] = turned[part : part + rows, :]
    for k in range(keep.shape[0]):
        keep[k] = held[me[1] ^ (2 * k)]
        send[k] = held[me[1] ^ (2 * k + 1)]


def pair_kernel(keep, got, *outs):
    for k, out in enumerate(outs):
        out[0] = keep[k]
        out[1] = got[k]


def stack_kernel(*refs):
    for k, part in enumerate(refs[:-1]):
        refs[-1][2 * k] = part[0]
        refs[-1][2 * k + 1] = part[1]


def weight_kernel(plan, me, all_c, *refs):
    features, out = refs[:-1], refs[-1]
    rows = out.shape[1]
    for k, blocks in plan:
        total = None
        for index, begin in blocks:
            for j in range(features[index].shape[0]):
                term = dot(features[index][j], all_c[me[1] ^ (begin + j)])
                total = term if total is None else total + term
        count = total.shape[0] // rows
        for q in range(count):
            out[(me[2] ^ k) * count + q] = total[q * rows : (q + 1) * rows].astype(bf16)


def intra_kernel(cum, x, dy, b, c, skip, dxp, xt, dye, dc, db, dcum, rows):
    heads = skip.shape[1]
    total = cum[...]
    tail = jnp.exp(total[SPAN - 1 :, :] - total)
    grow = jnp.exp(total)
    total_t = total.T
    keep = iota((SPAN, SPAN), 1) >= iota((SPAN, SPAN), 0)
    lane = iota((SPAN, SPAN), 1)
    first = first_head()
    gain = skip[...]
    mask_a = jnp.where(first, 1.0, 0.0).astype(bf16)
    mask_b = jnp.where(first, 0.0, 1.0).astype(bf16)
    gram_t = dot_nt(b[...], c[...])
    dgram_t = jnp.zeros((SPAN, SPAN), f32)
    columns = jnp.zeros((SPAN, SPAN), f32)
    rows[...] = jnp.zeros_like(rows)
    for j in range(heads // 2):
        lanes = slice(j * PAIR, (j + 1) * PAIR)
        x_pair, dy_pair = x[:, lanes], dy[:, lanes]
        x_two = jnp.concatenate([x_pair * mask_a, x_pair * mask_b], axis=0)
        dy_two = jnp.concatenate([dy_pair * mask_a, dy_pair * mask_b], axis=0)
        dm_two = dot_nt(x_two, dy_pair)
        mixes = []
        for k in range(2):
            h = 2 * j + k
            dm = dm_two[k * SPAN : (k + 1) * SPAN]
            diff = total_t[h : h + 1, :] - total[:, h : h + 1]
            w = jnp.exp(jnp.where(keep, jnp.minimum(diff, 0.0), -1e30))
            wd = w * dm
            dgram_t = dgram_t + wd
            q = wd * gram_t
            columns = jnp.where(lane == h, jnp.sum(q, axis=1, keepdims=True), columns)
            rows[h : h + 1, :] = jnp.sum(q, axis=0, keepdims=True)
            mixes.append((w * gram_t).astype(bf16))
        dx = dot(jnp.concatenate(mixes, axis=1), dy_two)
        dy_wide = dy_pair.astype(f32)
        dxp[:, lanes] = dx + spread(gain, j, first) * dy_wide
        xt[:, lanes] = (x_pair.astype(f32) * spread(tail, j, first)).astype(bf16)
        dye[:, lanes] = (dy_wide * spread(grow, j, first)).astype(bf16)
    dcum[...] = rows[...].T - columns
    high = dgram_t.astype(bf16)
    dc[...] = dot(high.astype(f32).T.astype(bf16), b[...])
    db[...] = dot(high, c[...])


def grad_c_kernel(dc, dye, starts, grad_c, copies):
    total = dc[...]
    pieces, width = starts.shape[0], starts.shape[2]
    for j in range(pieces):
        total = total + dot_nt(dye[:, j * width : (j + 1) * width], starts[j])
    out = total.astype(bf16)
    grad_c[...] = out
    for k in range(copies.shape[0]):
        copies[k] = out


def halves(a):
    high = a.astype(bf16)
    return high, (a - high.astype(f32)).astype(bf16)


def rest_kernel(
    me, starts, end_a, end_b, end_c, end_d, x, dy, xt, cum, loga, onehot, b, c, dxp, db, dcum, grad_x, grad_b, small, ends
):
    heads = x.shape[1] // P_SIZE
    pairs_piece = starts.shape[2] // PAIR
    for k, part in enumerate((end_a, end_b, end_c, end_d)):
        ends[(me[0] % GROUP) ^ k] = part[...]
    total = cum[...]
    last = total[SPAN - 1 :, :]
    tail = jnp.exp(last - total)
    grow = jnp.exp(total)
    end = jnp.exp(last)
    first = first_head()
    row = iota((SPAN, PAIR), 0)
    lane_head = iota((PAIR, 128), 0) // P_SIZE
    column = iota((PAIR, 128), 1)
    b_total = db[...]
    d_total = dcum[...]
    skips = jnp.zeros((8, 128), f32)
    for j in range(heads // 2):
        piece, at = j // pairs_piece, j % pairs_piece * PAIR
        lanes = slice(j * PAIR, (j + 1) * PAIR)
        start, stop = starts[piece, :, at : at + PAIR], ends[piece, :, at : at + PAIR]
        xs = xt[:, lanes]
        x_wide, dy_wide = x[:, lanes].astype(f32), dy[:, lanes].astype(f32)
        falling = spread(tail, j, first)
        carried = dy_wide * spread(grow, j, first) * dot(c[...], start)
        back = falling * dot(b[...], stop)
        left = x_wide * back
        grad_x[:, lanes] = (dxp[:, lanes] + back).astype(bf16)
        b_total = b_total + dot_nt(xs, stop)
        at_end = jnp.sum(left, axis=0, keepdims=True) + spread(end, j, first) * jnp.sum(
            start.astype(f32) * stop.astype(f32), axis=0, keepdims=True
        )
        moved = carried - left + jnp.where(row == SPAN - 1, at_end, 0.0)
        skip = jnp.sum(x_wide * dy_wide, axis=0, keepdims=True)
        skip = jnp.broadcast_to(skip, (8, PAIR))
        to_head = jnp.where(column == 2 * j + lane_head, 1.0, 0.0).astype(bf16)
        to_skip = jnp.where(column == heads + 2 * j + lane_head, 1.0, 0.0).astype(bf16)
        high, low = halves(moved)
        d_total = d_total + dot(high, to_head) + dot(low, to_head)
        high, low = halves(skip)
        skips = skips + dot(high, to_skip) + dot(low, to_skip)
    grad_b[...] = b_total.astype(bf16)
    upper = (iota((SPAN, SPAN), 1) >= iota((SPAN, SPAN), 0)).astype(f32)
    dlog = jnp.dot(upper, d_total, precision=HIGHEST, preferred_element_type=f32)
    rates = jnp.sum(dlog * loga[...], axis=0, keepdims=True)
    small[...] = onehot[...] * rates + jnp.where(iota((8, 128), 0) == 0, skips, 0.0)


def shard_kernel(parts, small, shard, copies):
    total = jnp.sum(parts[...].astype(f32), axis=0)
    shard[...] = total
    square = jnp.sum(total * total)
    here = (iota((8, 128), 0) == 0) & (iota((8, 128), 1) == 127)
    out = small[...] + jnp.where(here, square, 0.0)
    for k in range(copies.shape[0]):
        copies[k] = out


def sum_kernel(got, copies):
    out = jnp.sum(got[...], axis=0)
    for k in range(copies.shape[0]):
        copies[k] = out


def update_kernel(streams, size, me, got, shard, weight, moment_one, moment_two, new_w, new_m, new_s, rates, skips):
    total = jnp.sum(got[...], axis=0)
    mine = got[me[2] * streams]
    for k in range(1, streams):
        mine = mine + got[me[2] * streams + k]
    here = (iota((8, 128), 0) == 0) & (iota((8, 128), 1) == 127)
    square = jnp.sum(jnp.where(here, total, 0.0), keepdims=True)
    heads = rates.shape[1]
    rates[...] = mine[: rates.shape[0], :heads]
    skips[...] = mine[0:1, heads : 2 * heads]
    limit = 0.25 * math.sqrt(size)
    clipped = shard[...] * (limit / jnp.maximum(jnp.sqrt(square), limit))
    moment = beta_one * moment_one[...] + (1.0 - beta_one) * clipped
    second = beta_two * moment_two[...] + (1.0 - beta_two) * clipped * clipped
    direction = (
        moment
        / (1.0 - beta_one**step_count)
        / (jnp.sqrt(second / (1.0 - beta_two**step_count)) + adam_eps)
    )
    new_w[...] = weight[...] - learn_rate * (direction + decay_weight * weight[...])
    new_m[...] = moment
    new_s[...] = second


def call(kernel, out_shapes, *args, scratch=(), flops=0, limit=32, hbm=(), stay=()):
    size = sum(math.prod(a.shape) * a.dtype.itemsize for a in (*args, *out_shapes))
    whole = pl.BlockSpec(memory_space=pltpu.VMEM)
    scalars = pl.BlockSpec(memory_space=pltpu.SMEM)
    far = pl.BlockSpec(memory_space=pltpu.HBM)
    count = len(out_shapes)
    args = [
        pltpu.with_memory_space_constraint(a, pltpu.HBM) if at in stay else a
        for at, a in enumerate(args)
    ]

    def body(*refs):
        ins, rest = refs[: len(args)], refs[len(args) :]
        outs, own, held = rest[:count], rest[count : count + len(scratch)], rest[count + len(scratch) :]
        shown = list(outs)
        for k, at in enumerate(hbm):
            shown[at] = held[k]
        kernel(*ins, *shown, *own)
        copies = [
            pltpu.make_async_copy(held[k], outs[at], held[-1].at[k]) for k, at in enumerate(hbm)
        ]
        for copy in copies:
            copy.start()
        for copy in copies:
            copy.wait()

    held = [pltpu.VMEM(out_shapes[at].shape, out_shapes[at].dtype) for at in hbm]
    if hbm:
        held.append(pltpu.SemaphoreType.DMA((len(hbm),)))
    out = pl.pallas_call(
        body,
        out_shape=tuple(
            pltpu.HBM(o.shape, o.dtype) if at in hbm else o for at, o in enumerate(out_shapes)
        ),
        in_specs=[
            far if at in stay else scalars if a.shape == (3,) else whole
            for at, a in enumerate(args)
        ],
        out_specs=tuple(
            far if at in hbm else whole for at in range(count)
        ),
        scratch_shapes=[*scratch, *held],
        compiler_params=pltpu.CompilerParams(vmem_limit_bytes=limit * 1024 * 1024),
        cost_estimate=pl.CostEstimate(flops=flops, bytes_accessed=size, transcendentals=0),
    )(*args)
    return out[0] if count == 1 else out


def shaped(shape, dtype):
    return jax.ShapeDtypeStruct(shape, dtype)


def swap(a, axis, groups=None):
    return lax.all_to_all(a, axis, 0, 0, tiled=True, axis_index_groups=groups)


def trade(a, axis, k):
    count = lax.axis_size(axis)
    return lax.ppermute(a, axis, [(i, i ^ k) for i in range(count)])


def local(
    seq_values,
    proj_b,
    proj_c,
    time_step,
    decay_level,
    decay_rate,
    skip_gain,
    grad_out,
    layer_input,
    weight_c,
    moment_one,
    moment_two,
):
    seqs, streams, tensors = (lax.axis_size(a) for a in ("seq", "dp", "tensor"))
    me = jnp.stack([lax.axis_index(a) for a in ("seq", "dp", "tensor")]).astype(jnp.int32)
    x, dy, b, c = seq_values[0], grad_out[0], proj_b[0], proj_c[0]
    heads = skip_gain.shape[0]
    width = heads * P_SIZE
    piece = width // GROUP
    near = [[i + k for k in range(GROUP)] for i in range(0, seqs, GROUP)]
    far = [list(range(i, seqs, GROUP)) for i in range(GROUP)]
    tile = shaped((SPAN, 128), f32)
    small_tile = shaped((8, 128), f32)
    wide = shaped((SPAN, width), bf16)
    st, loga, cum, onehot = call(
        states_kernel,
        [shaped((GROUP, 2 * N + LOG_ROWS, piece), bf16), tile, tile, small_tile],
        time_step[0].T,
        decay_level[0],
        decay_rate.T,
        x,
        dy,
        b,
        c,
        flops=4 * SPAN * N * width,
        limit=60,
    )
    layer, st = lax.optimization_barrier((layer_input[0], st))
    got = swap(st, "seq", near)

    rows = weight_c.shape[0]
    block = layer.shape[1] // streams
    half = max(streams // 2, 1)
    keep, send = call(
        functools.partial(feature_kernel, rows),
        [shaped((half, block, SPAN), bf16)] * 2,
        me,
        layer,
        scratch=[pltpu.VMEM((streams, block, SPAN), bf16)],
    )
    pairs = call(
        pair_kernel, [shaped((2, block, SPAN), bf16)] * half, keep, trade(send, "dp", 1)
    )
    pairs = [pairs] if half == 1 else pairs
    pairs = [pairs[0]] + [trade(pairs[k], "dp", 2 * k) for k in range(1, half)]
    got, *pairs = lax.optimization_barrier((got, *pairs))
    mine = call(stack_kernel, [shaped((streams, block, SPAN), bf16)], *pairs)
    left, right = trade(mine, "tensor", 1), trade(mine, "tensor", 3)

    dxp, xt, dye, dc, db, dcum = call(
        intra_kernel,
        [shaped((SPAN, width), f32), wide, wide, tile, tile, tile],
        cum,
        x,
        dy,
        b,
        c,
        skip_gain[None],
        scratch=[pltpu.VMEM((SPAN, SPAN), f32)],
        flops=20 * SPAN * SPAN * width,
        hbm=(0, 1, 2, 4, 5),
    )
    ahead = call(
        group_kernel,
        [shaped((seqs // GROUP, N + LOG_ROWS, piece), bf16)],
        me,
        got,
        flops=8 * N * width,
    )
    groups = swap(ahead, "seq", far)
    groups, left, right = lax.optimization_barrier((groups, left, right))
    far_a = trade(right[:half], "tensor", 1)
    far_b = trade(left[half:], "tensor", 3)
    plan = ((0, ((0, 0),)), (1, ((1, 0),)), (3, ((2, 0),)), (2, ((3, 0), (4, half))))
    starts, *ends = call(
        scan_kernel,
        [shaped((GROUP, N, piece), bf16)] + [shaped((N, piece), bf16)] * GROUP,
        me,
        got,
        groups,
        scratch=[pltpu.VMEM((GROUP, N, piece), bf16)],
        flops=8 * N * width,
        hbm=range(GROUP + 1),
    )
    starts = swap(starts, "seq", near)
    starts, far_a, far_b = lax.optimization_barrier((starts, far_a, far_b))
    grad_c, copies = call(
        grad_c_kernel,
        [shaped((SPAN, N), bf16), shaped((streams, SPAN, N), bf16)],
        dc,
        dye,
        starts,
        flops=2 * SPAN * N * width,
    )
    copies, *ends = lax.optimization_barrier((copies, *ends))
    all_c = swap(copies, "dp")
    ends = [ends[0]] + [trade(ends[k], "seq", k) for k in range(1, GROUP)]
    all_c, *ends = lax.optimization_barrier((all_c, *ends))
    partial = call(
        functools.partial(weight_kernel, plan),
        [shaped((seqs, rows, N), bf16)],
        me,
        all_c,
        mine,
        left,
        right,
        far_a,
        far_b,
        flops=2 * tensors * layer.shape[1] * SPAN * N,
    )
    parts = swap(partial, "seq")
    grad_x, grad_b, small = call(
        rest_kernel,
        [wide, shaped((SPAN, N), bf16), small_tile],
        me,
        starts,
        *ends,
        x,
        dy,
        xt,
        cum,
        loga,
        onehot,
        b,
        c,
        dxp,
        db,
        dcum,
        scratch=[pltpu.VMEM((GROUP, N, piece), bf16)],
        flops=6 * SPAN * N * width,
    )
    shard, sums = call(
        shard_kernel,
        [shaped((rows, N), f32), shaped((seqs, 8, 128), f32)],
        parts,
        small,
        flops=seqs * rows * N,
    )
    sums = call(sum_kernel, [shaped((tensors * streams, 8, 128), f32)], swap(sums, "seq"))
    matrix = shaped((rows, N), f32)
    size = rows * seqs * streams * N * tensors
    new_weight, new_moment, new_second, rates, skips = call(
        functools.partial(update_kernel, streams, size),
        [matrix, matrix, matrix, shaped((decay_rate.shape[1], heads), f32), shaped((1, heads), f32)],
        me,
        swap(sums, ("tensor", "dp")),
        shard,
        weight_c,
        moment_one,
        moment_two,
    )
    return (
        grad_x[None],
        grad_b[None],
        grad_c[None],
        rates.T,
        skips[0],
        new_weight,
        new_moment,
        new_second,
    )


def solution(mesh):
    wide = P("dp", "seq", "tensor")
    shard = P(("seq", "dp"), "tensor")
    return jax.shard_map(
        local,
        mesh=mesh,
        in_specs=(
            wide,
            wide,
            wide,
            wide,
            wide,
            P("tensor", None),
            P("tensor"),
            wide,
            wide,
            shard,
            shard,
            shard,
        ),
        out_specs=(wide, wide, wide, P("tensor", None), P("tensor"), shard, shard, shard),
        check_vma=False,
    )
```
